128 devices in a mesh: ctx: 8 (over x, core), fsdp: 16 (over z, y).
Axes of the slice: x: 4, y: 4, z: 4, core: 2. Of those that a mesh axis runs over, the one named last changes fastest.
Arguments:
- tokens: bfloat16 [16, 16, 128, 768], P('fsdp', 'ctx'), may hold values from -6 to 6
- dealing: int32 [16, 16], P('fsdp'), may hold values from 0 to 15, each once within a row
- qkv_weight: bfloat16 [768, 2304], P('fsdp'), may hold values from -0.21875 to 0.21875
- ln1_gain: bfloat16 [768], P('fsdp'), may hold values from 0.5 to 1.5
- ln1_bias: bfloat16 [768], P('fsdp'), may hold values from -1 to 1
- q_bias: bfloat16 [768], P('fsdp'), may hold values from -0.5 to 0.5
- v_bias: bfloat16 [768], P('fsdp'), may hold values from -0.14941406 to 0.14941406
- out_weight: bfloat16 [768, 768], P('fsdp'), may hold values from -9.75 to 9.75
- out_bias: bfloat16 [768], P('fsdp'), may hold values from -1 to 1
- ln2_gain: bfloat16 [768], P('fsdp'), may hold values from 0.5 to 1.5
- ln2_bias: bfloat16 [768], P('fsdp'), may hold values from -1 to 1
- fc_weight: bfloat16 [3072, 768], P('fsdp'), may hold values from -0.21875 to 0.21875
- fc_bias: bfloat16 [3072], P('fsdp'), may hold values from -1 to 1
- proj_weight: bfloat16 [3072, 768], P('fsdp'), may hold values from -0.109375 to 0.109375
- proj_bias: bfloat16 [768], P('fsdp'), may hold values from -1 to 1
- cotangent: bfloat16 [16, 16, 128, 768], P('fsdp', 'ctx'), may hold values from -6 to 6
Outputs:
- output: bfloat16 [16, 16, 128, 768], P('fsdp', 'ctx')
- token_grad: float32 [16, 16, 128, 768], P('fsdp', 'ctx')
- qkv_weight_grad: float32 [768, 2304], P('fsdp')
- ln1_gain_grad: float32 [768], P('fsdp')
- ln1_bias_grad: float32 [768], P('fsdp')
- q_bias_grad: float32 [768], P('fsdp')
- v_bias_grad: float32 [768], P('fsdp')
- out_weight_grad: float32 [768, 768], P('fsdp')
- out_bias_grad: float32 [768], P('fsdp')
- ln2_gain_grad: float32 [768], P('fsdp')
- ln2_bias_grad: float32 [768], P('fsdp')
- fc_weight_grad: float32 [3072, 768], P('fsdp')
- hidden_bias_gradient: float32 [3072], P('fsdp')
- proj_weight_grad: float32 [3072, 768], P('fsdp')
- proj_bias_grad: float32 [768], P('fsdp')
The draws below stay inside these ranges and needn't reach their ends.
Inputs may be any that keep to these rules, and one draw needn't show every extreme that they name: Each row of dealing names every causal block of its sequence once.
All inputs are finite; a program needn't handle non-finite values.
Results may differ from the reference program's by a relative error of at most 0.022.
Values may be sent and summed in bfloat16 or wider, within the bound.
No kernel may reach another device: no remote copies, remote signals or barrier semaphores. Data moves between devices by JAX's collectives and lax.ppermute only.
A program may use at most 192 MiB of HBM per device.

```python
import jax
import jax.numpy as jnp
from jax import lax

MODEL_DIM = 768
HEADS = 12
HD = 64
FF = 3072
BLOCK_TOKENS = 128
CAUSAL_BLOCKS = 16
SEQ = 2048
SEQUENCE_COUNT = 16


def level_of(key, shape, cuts, least, largest):
    def one(axis_at, blocks):
        draws = jax.random.uniform(jax.random.fold_in(jax.random.fold_in(key, 6), axis_at), (blocks,), jnp.float32, least / len(cuts), largest / len(cuts))
        return jnp.repeat(jnp.exp(draws), shape[axis_at] // blocks).reshape((-1,) + (1,) * (len(shape) - axis_at - 1))

    factor_of = one(*cuts[0])
    for cut in cuts[1:]:
        factor_of = factor_of * one(*cut)
    return factor_of


def scatter_about(stream_key, shape, width, limit, cuts=(), kind=jnp.bfloat16):
    factor_of = level_of(stream_key, shape, cuts, -0.22, 0.18) if cuts else 1.0
    result = jax.random.normal(stream_key, shape, jnp.float32) * width * factor_of
    return jnp.minimum(jnp.maximum(result, -limit), limit).astype(kind)


def setup_inputs(seed: int = 0) -> dict:
    key_of = jax.random.split(jax.random.key(seed), 17)
    tokens = scatter_about(key_of[0], (SEQUENCE_COUNT, CAUSAL_BLOCKS, BLOCK_TOKENS, MODEL_DIM), 1.0, 6.0, ((0, 16), (1, 8)))
    dealing = jax.vmap(lambda own: jax.random.permutation(own, CAUSAL_BLOCKS))(jax.random.split(key_of[1], SEQUENCE_COUNT)).reshape((SEQUENCE_COUNT, CAUSAL_BLOCKS)).astype(jnp.int32)
    qkv_weight = scatter_about(key_of[2], (MODEL_DIM, 3 * MODEL_DIM), MODEL_DIM ** -0.5, 0.21875, ((0, 16),))
    ln1_gain = jnp.clip(1.0 + 0.1 * jax.random.normal(key_of[3], (MODEL_DIM,), jnp.float32), 0.5, 1.5).astype(jnp.bfloat16)
    ln1_bias = scatter_about(key_of[4], (MODEL_DIM,), 0.2, 1.0, ((0, 16),))
    q_bias = scatter_about(key_of[5], (MODEL_DIM,), 0.1, 0.5, ((0, 16),))
    v_bias = scatter_about(key_of[6], (MODEL_DIM,), 0.03, 0.14941406, ((0, 16),))
    out_weight = scatter_about(key_of[7], (MODEL_DIM, MODEL_DIM), ((SEQ / MODEL_DIM) ** 0.5 / 2), 9.75, ((0, 16),))
    out_bias = scatter_about(key_of[8], (MODEL_DIM,), 0.2, 1.0, ((0, 16),))
    ln2_gain = jnp.clip(1.0 + 0.1 * jax.random.normal(key_of[9], (MODEL_DIM,), jnp.float32), 0.5, 1.5).astype(jnp.bfloat16)
    ln2_bias = scatter_about(key_of[10], (MODEL_DIM,), 0.2, 1.0, ((0, 16),))
    fc_weight = scatter_about(key_of[11], (FF, MODEL_DIM), MODEL_DIM ** -0.5, 0.21875, ((0, 16),))
    fc_bias = scatter_about(key_of[12], (FF,), 0.2, 1.0, ((0, 16),))
    proj_weight = scatter_about(key_of[13], (FF, MODEL_DIM), FF ** -0.5, 0.109375, ((0, 16),))
    proj_bias = scatter_about(key_of[14], (MODEL_DIM,), 0.2, 1.0, ((0, 16),))
    cotangent = scatter_about(key_of[15], (SEQUENCE_COUNT, CAUSAL_BLOCKS, BLOCK_TOKENS, MODEL_DIM), 1.0, 6.0, ((0, 16), (1, 8)))
    return dict(tokens=tokens, dealing=dealing, qkv_weight=qkv_weight, ln1_gain=ln1_gain, ln1_bias=ln1_bias, q_bias=q_bias, v_bias=v_bias, out_weight=out_weight, out_bias=out_bias, ln2_gain=ln2_gain, ln2_bias=ln2_bias, fc_weight=fc_weight, fc_bias=fc_bias, proj_weight=proj_weight, proj_bias=proj_bias, cotangent=cotangent)


@jax.custom_vjp
def low(v):
    return lax.optimization_barrier(v.astype(jnp.bfloat16)).astype(jnp.float32)

@jax.custom_vjp
def low_back(v):
    return v

def low_keep(v):
    return (low(v), None)

def low_pass(kept, grad):
    return (grad,)

def back_keep(v):
    return (v, None)

def back_low(kept, grad):
    return (low(grad),)
low.defvjp(low_keep, low_pass)
low_back.defvjp(back_keep, back_low)

def matmul(left_side, right_side):
    return jnp.dot(left_side, right_side, precision=lax.Precision.HIGHEST, preferred_element_type=jnp.float32)

def layer_norm(values, gain_vector, bias_vector):
    centre = values - lax.optimization_barrier(jnp.mean(values, axis=-1, keepdims=True))
    spread = lax.optimization_barrier(jnp.mean(centre * centre, axis=-1, keepdims=True))
    return centre * lax.rsqrt(spread + 1e-05) * gain_vector + bias_vector

def one_sequence(params, tokens_seq, deal_row):
    qkv_weight, ln1_gain, ln1_bias, q_bias, v_bias, out_weight, out_bias, ln2_gain, ln2_bias, fc_weight, fc_bias, proj_weight, proj_bias = params
    flat_rows = tokens_seq.reshape(SEQ, MODEL_DIM)
    places = (deal_row[:, None] * BLOCK_TOKENS + jnp.arange(BLOCK_TOKENS, dtype=jnp.int32)[None, :]).reshape(SEQ)
    normed = low(layer_norm(flat_rows, ln1_gain, ln1_bias))
    projected = matmul(normed, qkv_weight)
    queries = low(low_back(projected[:, :MODEL_DIM] + q_bias)).reshape(SEQ, HEADS, HD)
    keys_low = low(low_back(projected[:, MODEL_DIM:2 * MODEL_DIM])).reshape(SEQ, HEADS, HD)
    values_low = low(low_back(projected[:, 2 * MODEL_DIM:] + v_bias)).reshape(SEQ, HEADS, HD)
    scores = jnp.einsum('qhd,khd->hqk', queries, keys_low, precision=lax.Precision.HIGHEST) * HD ** (-0.5)
    scores = low_back(scores)
    allowed = places[None, :] <= places[:, None]
    masked = jnp.where(allowed[None], scores, -1e+30)
    peak = lax.optimization_barrier(jnp.max(masked, axis=-1, keepdims=True))
    raw_weights = jnp.exp(masked - peak)
    row_total = lax.optimization_barrier(jnp.sum(raw_weights, axis=-1, keepdims=True))
    attended = jnp.einsum('hqk,khd->hqd', low(raw_weights), values_low, precision=lax.Precision.HIGHEST) / row_total
    attended = jnp.transpose(attended, (1, 0, 2)).reshape(SEQ, MODEL_DIM)
    attended = low(low_back(attended))
    residual = flat_rows + low_back(matmul(attended, out_weight) + out_bias)
    normed_two = low(layer_norm(residual, ln2_gain, ln2_bias))
    hidden = low_back(matmul(normed_two, fc_weight.T) + fc_bias)
    active = low(jax.nn.gelu(hidden, approximate=True))
    layer_result = residual + matmul(active, proj_weight) + proj_bias
    return layer_result.reshape(CAUSAL_BLOCKS, BLOCK_TOKENS, MODEL_DIM)

def whole_layer(tokens, dealing, params):
    per_sequence = jax.checkpoint(lambda element: one_sequence(params, element[0], element[1]))
    return lax.map(per_sequence, (tokens, dealing))

def reference(tokens, dealing, qkv_weight, ln1_gain, ln1_bias, q_bias, v_bias, out_weight, out_bias, ln2_gain, ln2_bias, fc_weight, fc_bias, proj_weight, proj_bias, cotangent):
    params = tuple((p.astype(jnp.float32) for p in (qkv_weight, ln1_gain, ln1_bias, q_bias, v_bias, out_weight, out_bias, ln2_gain, ln2_bias, fc_weight, fc_bias, proj_weight, proj_bias)))

    def forward(inputs, *weights_all):
        return whole_layer(inputs, dealing, weights_all)
    layer_result, pullback = jax.vjp(forward, tokens.astype(jnp.float32), *params)
    gradients = pullback(cotangent.astype(jnp.float32))
    return (layer_result.astype(jnp.bfloat16), gradients[0], gradients[1], gradients[2], gradients[3], gradients[4], gradients[5], gradients[6], gradients[7], gradients[8], gradients[9], gradients[10], gradients[11], gradients[12], gradients[13])
```

```python
import jax
import jax.numpy as jnp
from jax import lax
from jax.experimental import pallas as pl
from jax.experimental.pallas import tpu as pltpu
from jax.sharding import Mesh, PartitionSpec as P

D = 768
FF = 3072
HC = 3
HD = 64
CH = HC * HD
BT = 128
SEQ = 2048
ROWS = 256
KC = 512
EPS = 1e-05
NEG = -1e30
F32 = jnp.float32
BF16 = jnp.bfloat16

NT = (((1,), (1,)), ((), ()))
TN = (((0,), (0,)), ((), ()))


def dot(a, b):
    return jnp.dot(a, b, preferred_element_type=F32)


def dot_nt(a, b):
    return lax.dot_general(a, b, NT, preferred_element_type=F32)


def dot_tn(a, b):
    return lax.dot_general(a, b, TN, preferred_element_type=F32)


def standardize(v):
    centre = v - jnp.mean(v, axis=-1, keepdims=True)
    spread = jnp.mean(centre * centre, axis=-1, keepdims=True)
    root = lax.rsqrt(spread + EPS)
    return centre * root, root


def rel(a, b):
    return lax.rem(a - b + 4, 4)


def forward_kernel(meta, *refs):
    toks = refs[0:8]
    wrel = refs[8:12]
    vec, qvb = refs[12:14]
    (atts, attt_ref, lse_ref, q_ref, k_ref, kt_ref, v_ref, normed_ref, w_ref) = (
        refs[14:18],
        *refs[18:26],
    )
    vt_ref = refs[26]
    z, y = meta[2], meta[3]
    for ky in range(4):
        for kz in range(4):
            shard = rel(z, kz) * 4 + rel(y, ky)
            w_ref[pl.ds(pl.multiple_of(shard * 48, 16), 48), :] = wrel[ky][kz * 64 : kz * 64 + 48, :]
    gain = vec[0:1, :]
    bias = vec[1:2, :]
    qb = qvb[0:1, :]
    vb = qvb[1:2, :]
    w = w_ref[...]
    for k in range(8):
        own = k < 4
        xhat, _ = standardize(toks[k][...].astype(F32))
        normed = (xhat * gain + bias).astype(BF16)
        if own:
            normed_ref[k * ROWS : (k + 1) * ROWS, :] = normed
            proj = dot(normed, w)
            q = (proj[:, :CH] + qb).astype(BF16) * jnp.asarray(HD**-0.5, BF16)
            for h in range(HC):
                q_ref[h, k * ROWS : (k + 1) * ROWS, :] = q[:, h * HD : (h + 1) * HD]
            kv = proj[:, CH:]
        else:
            kv = dot(normed, w[:, CH:])
        for r in range(2):
            place = pl.multiple_of(meta[4 + 2 * k + r] * BT, BT)
            kk = kv[r * BT : (r + 1) * BT, :CH]
            vv = kv[r * BT : (r + 1) * BT, CH:] + vb
            kb = kk.astype(BF16)
            vbl = vv.astype(BF16)
            for h in range(HC):
                cols = slice(h * HD, (h + 1) * HD)
                k_ref[h, pl.ds(place, BT), :] = kb[:, cols]
                v_ref[h, pl.ds(place, BT), :] = vbl[:, cols]
                kt_ref[h, :, pl.ds(place, BT)] = kk[:, cols].T.astype(BF16)
                vt_ref[h, :, pl.ds(place, BT)] = vv[:, cols].T.astype(BF16)

    key_iota = lax.broadcasted_iota(jnp.int32, (KC, BT), 0)
    query_iota = lax.broadcasted_iota(jnp.int32, (KC, BT), 1)
    for i in range(8):
        pos = meta[4 + i]
        queries = [q_ref[h, i * BT : (i + 1) * BT, :] for h in range(HC)]

        def step(j, carry, masked, pos=pos, queries=queries):
            base = pl.multiple_of(j * KC, KC)
            out = []
            if masked:
                keep = key_iota + base <= query_iota + pos * BT
            for h in range(HC):
                m, total, acc = carry[h]
                s = dot_nt(k_ref[h, pl.ds(base, KC), :], queries[h])
                if masked:
                    s = jnp.where(keep, s, NEG)
                m_new = jnp.maximum(m, jnp.max(s, axis=0, keepdims=True))
                e = jnp.exp(s - m_new)
                a = jnp.exp(m - m_new)
                total = total * a + jnp.sum(e, axis=0, keepdims=True)
                acc = acc * a + dot(vt_ref[h, :, pl.ds(base, KC)], e.astype(BF16))
                out.append((m_new, total, acc))
            return tuple(out)

        full = lax.div(pos * BT, KC)
        carry = tuple(
            (jnp.full((1, BT), NEG, F32), jnp.zeros((1, BT), F32), jnp.zeros((HD, BT), F32))
            for _ in range(HC)
        )
        carry = lax.fori_loop(0, full, lambda j, c: step(j, c, False), carry)
        carry = step(full, carry, True)
        parts = []
        for h in range(HC):
            m, total, acc = carry[h]
            att = acc / total
            attt_ref[i, h] = att
            lse_ref[i, h : h + 1, :] = m + jnp.log(total)
            parts.append(att.T.astype(BF16))
        for h in range(HC):
            atts[i // 2][(i % 2) * BT : (i % 2 + 1) * BT, h * HD : (h + 1) * HD] = parts[h]


def gelu_parts(v):
    c = 0.7978845608028654
    t = jnp.tanh(c * (v + 0.044715 * (v * v * v)))
    act = 0.5 * v * (1.0 + t)
    slope = 0.5 * (1.0 + t) + (0.5 * c) * v * (1.0 - t * t) * (1.0 + (3 * 0.044715) * v * v)
    return act, slope


def mlp_kernel(
    meta,
    a0,
    a1,
    a2,
    a3,
    tok,
    cot,
    wout,
    vec,
    fcb,
    wblk,
    out_ref,
    gm_ref,
    d0,
    d1,
    d2,
    d3,
    own_a,
    own_b,
    oth_a,
    oth_b,
    vg_ref,
    fcg_ref,
    middle_s,
    xhat_s,
    root_s,
    n2_s,
    ffn_s,
    dn_s,
    dout_s,
):
    j = pl.program_id(0)
    x, c, z, y = meta[0], meta[1], meta[2], meta[3]
    atts = (a0, a1, a2, a3)

    def head_rows(k):
        return pl.ds(pl.multiple_of(lax.rem(x + k, 4) * CH, 64), CH)

    @pl.when(j == 0)
    def _():
        branch = vec[4:5, :]
        middle = tok[...].astype(F32)
        for k in range(4):
            middle = middle + dot(atts[k][...], wout[head_rows(k), :])
        middle = middle + branch
        xhat, root = standardize(middle)
        middle_s[...] = middle
        xhat_s[...] = xhat
        root_s[...] = root
        n2_s[...] = (xhat * vec[5:6, :] + vec[6:7, :]).astype(BF16)
        ffn_s[...] = jnp.zeros_like(ffn_s)
        dn_s[...] = jnp.zeros_like(dn_s)

    fc = wblk[:, 64:256, :].reshape(D, D)
    proj = wblk[:, 256:448, :].reshape(D, D)
    cols = pl.ds(pl.multiple_of(j * D, D), D)
    n2 = n2_s[...]
    ct = cot[...]
    hidden = dot_nt(n2, fc) + fcb[:, cols]
    act, slope = gelu_parts(hidden)
    act = act.astype(BF16)
    ffn_s[...] += dot(act, proj)
    gh = dot_nt(ct, proj) * slope
    gh = gh.astype(BF16)
    dn_s[...] += dot(gh, fc)
    fcg_ref[:, cols] = jnp.sum(gh.astype(F32), axis=0, keepdims=True)
    dproj = dot_tn(act, ct).astype(BF16)
    dfc = dot_tn(gh, n2).astype(BF16)
    kz = rel(j, z)
    for yy in range(4):
        ky = rel(yy, y)
        first = slice(yy * 192, yy * 192 + 96)
        second = slice(yy * 192 + 96, (yy + 1) * 192)

        @pl.when(c == 0)
        def _():
            own_a[kz, ky, 0:96, :] = dfc[first]
            own_b[ky, kz, 0:96, :] = dfc[second]
            oth_a[kz, ky, 0:96, :] = dproj[first]
            oth_b[ky, kz, 0:96, :] = dproj[second]

        @pl.when(c == 1)
        def _():
            oth_a[kz, ky, 0:96, :] = dfc[first]
            oth_b[ky, kz, 0:96, :] = dfc[second]
            own_a[kz, ky, 0:96, :] = dproj[first]
            own_b[ky, kz, 0:96, :] = dproj[second]

    @pl.when(j == 3)
    def _():
        ctf = ct.astype(F32)
        out_ref[...] = (middle_s[...] + ffn_s[...] + vec[7:8, :]).astype(BF16)
        dn = dn_s[...]
        xhat = xhat_s[...]
        e = dn * vec[5:6, :]
        part = e - jnp.mean(e, axis=-1, keepdims=True)
        part = part - xhat * jnp.mean(e * xhat, axis=-1, keepdims=True)
        gm = ctf + part * root_s[...]
        gm_ref[...] = gm
        gb = gm.astype(BF16)
        zero = jnp.zeros((4, D), F32)
        vg_ref[...] = jnp.concatenate(
            [
                jnp.sum(gb.astype(F32), axis=0, keepdims=True),
                jnp.sum(dn * xhat, axis=0, keepdims=True),
                jnp.sum(dn, axis=0, keepdims=True),
                jnp.sum(ctf, axis=0, keepdims=True),
                zero,
            ],
            axis=0,
        )
        for k, d in enumerate((d0, d1, d2, d3)):
            d[...] = dot_nt(gb, wout[head_rows(k), :]).astype(BF16)
            dout_s[head_rows(k), :] = dot_tn(atts[k][...], gb).astype(BF16)
        blank = jnp.zeros((16, D), BF16)
        for s in range(16):
            sz, sy = rel(s // 4, z), rel(s % 4, y)
            u = [dout_s[s * 48 + 16 * t : s * 48 + 16 * (t + 1), :] for t in range(3)]

            @pl.when(c == 0)
            def _():
                own_a[sz, sy, 96:112, :] = u[0]
                own_b[sy, sz, 96:112, :] = u[1]
                oth_a[sz, sy, 96:112, :] = u[2]
                oth_b[sy, sz, 96:112, :] = blank

            @pl.when(c == 1)
            def _():
                oth_a[sz, sy, 96:112, :] = u[0]
                oth_b[sy, sz, 96:112, :] = u[1]
                own_a[sz, sy, 96:112, :] = u[2]
                own_b[sy, sz, 96:112, :] = blank


def backward_kernel(meta, *refs):
    dos = refs[0:4]
    q_ref, k_ref, kt_ref, v_ref, attt_ref, lse_ref = refs[4:10]
    dq_ref, own_ref, oth_ref = refs[10:13]
    dk_s, dv_s, do_s = refs[13:16]
    dk_s[...] = jnp.zeros_like(dk_s)
    dv_s[...] = jnp.zeros_like(dv_s)
    for k in range(4):
        do = dos[k][...]
        for h in range(HC):
            do_s[h, k * ROWS : (k + 1) * ROWS, :] = do[:, h * HD : (h + 1) * HD]
    key_iota = lax.broadcasted_iota(jnp.int32, (KC, BT), 0)
    query_iota = lax.broadcasted_iota(jnp.int32, (KC, BT), 1)
    for i in range(8):
        pos = meta[4 + i]
        queries = [q_ref[h, i * BT : (i + 1) * BT, :] for h in range(HC)]
        grads = [do_s[h, i * BT : (i + 1) * BT, :] for h in range(HC)]
        lses = [lse_ref[i, h : h + 1, :] for h in range(HC)]
        corrs = [
            jnp.sum(grads[h].astype(F32).T * attt_ref[i, h], axis=0, keepdims=True)
            for h in range(HC)
        ]

        def step(j, carry, masked, pos=pos, queries=queries, grads=grads, lses=lses, corrs=corrs):
            base = pl.multiple_of(j * KC, KC)
            keys = pl.ds(base, KC)
            if masked:
                keep = key_iota + base <= query_iota + pos * BT
            out = []
            for h in range(HC):
                s = dot_nt(k_ref[h, keys, :], queries[h])
                p = jnp.exp(s - lses[h])
                if masked:
                    p = jnp.where(keep, p, 0.0)
                dp = dot_nt(v_ref[h, keys, :], grads[h])
                ds = (p * (dp - corrs[h])).astype(BF16)
                dv_s[h, keys, :] += dot(p.astype(BF16), grads[h])
                dk_s[h, keys, :] += dot(ds, queries[h])
                out.append(carry[h] + dot(kt_ref[h, :, keys], ds))
            return tuple(out)

        full = lax.div(pos * BT, KC)
        carry = tuple(jnp.zeros((HD, BT), F32) for _ in range(HC))
        carry = lax.fori_loop(0, full, lambda j, c: step(j, c, False), carry)
        carry = step(full, carry, True)
        for h in range(HC):
            dq_ref[i * BT : (i + 1) * BT, h * HD : (h + 1) * HD] = (
                (carry[h] * HD**-0.5).T.astype(BF16)
            )
    for i in range(8):
        here = pl.ds(pl.multiple_of(meta[4 + i] * BT, BT), BT)
        there = pl.ds(pl.multiple_of(meta[12 + i] * BT, BT), BT)
        rows = slice(i * BT, (i + 1) * BT)
        for h in range(HC):
            own_ref[rows, h * HD : (h + 1) * HD] = dk_s[h, here, :]
            own_ref[rows, CH + h * HD : CH + (h + 1) * HD] = dv_s[h, here, :]
            oth_ref[rows, h * HD : (h + 1) * HD] = dk_s[h, there, :].astype(BF16)
            oth_ref[rows, CH + h * HD : CH + (h + 1) * HD] = dv_s[h, there, :].astype(BF16)


def input_grad_kernel(dq_ref, own_ref, recv_ref, w_ref, n0, n1, n2, n3, g_ref):
    g_ref[:, :CH] = dq_ref[...]
    g_ref[:, CH:] = (own_ref[...] + recv_ref[...].astype(F32)).astype(BF16)
    w = w_ref[...]
    for k, n in enumerate((n0, n1, n2, n3)):
        n[...] = dot_nt(g_ref[k * ROWS : (k + 1) * ROWS, :], w).astype(BF16)


def weight_grad_kernel(
    meta, normed_ref, g_ref, t0, t1, t2, t3, n0, n1, n2, n3, own_ref, oth_ref, vg_ref, qv_ref, dw_s
):
    c, z, y = meta[1], meta[2], meta[3]
    g = g_ref[...]
    dw_s[...] = dot_tn(normed_ref[...], g).astype(BF16)
    blank = jnp.zeros((16, HC * CH), BF16)
    for s in range(16):
        sz, sy = rel(s // 4, z), rel(s % 4, y)
        first = dw_s[s * 48 : s * 48 + 32, :]
        second = dw_s[s * 48 + 32 : s * 48 + 48, :]

        @pl.when(c == 0)
        def _():
            own_ref[sz, sy] = first
            oth_ref[sz, sy, 0:16, :] = second
            oth_ref[sz, sy, 16:32, :] = blank

        @pl.when(c == 1)
        def _():
            oth_ref[sz, sy] = first
            own_ref[sz, sy, 0:16, :] = second
            own_ref[sz, sy, 16:32, :] = blank

    gain = jnp.zeros((1, D), F32)
    bias = jnp.zeros((1, D), F32)
    for t, n in zip((t0, t1, t2, t3), (n0, n1, n2, n3)):
        xhat, _ = standardize(t[...].astype(F32))
        ng = n[...].astype(F32)
        gain = gain + jnp.sum(ng * xhat, axis=0, keepdims=True)
        bias = bias + jnp.sum(ng, axis=0, keepdims=True)
    vg_ref[0:1, :] = gain
    vg_ref[1:2, :] = bias
    qv_ref[...] = jnp.sum(g.astype(F32), axis=0, keepdims=True)


def token_grad_kernel(tok, gm, vec, n0, n1, n2, n3, out_ref):
    ng = n0[...].astype(F32) + n1[...].astype(F32) + n2[...].astype(F32) + n3[...].astype(F32)
    xhat, root = standardize(tok[...].astype(F32))
    e = ng * vec[0:1, :]
    part = e - jnp.mean(e, axis=-1, keepdims=True)
    part = part - xhat * jnp.mean(e * xhat, axis=-1, keepdims=True)
    out_ref[...] = gm[...] + part * root


def shift(v, axis, k):
    return lax.ppermute(v, axis, [(i, (i + k) % 4) for i in range(4)])


def swap(v):
    return lax.ppermute(v, "core", [(0, 1), (1, 0)])


def gather4(v, axis):
    return [v] + [shift(v, axis, k) for k in (1, 2, 3)]


def scatter4(pieces, axis):
    total = pieces[0].astype(F32)
    for k in (1, 2, 3):
        total = total + shift(pieces[k], axis, k).astype(F32)
    return total.astype(BF16)


def in_order(pieces, index):
    up = [pieces[0], pieces[3], pieces[2], pieces[1]]
    twice = jnp.stack(up + up)
    return lax.dynamic_slice_in_dim(twice, rel(0, index), 4, axis=0)


def call(kernel, outs, scratch=(), smem=True, **kw):
    specs = [pl.BlockSpec(memory_space=pltpu.VMEM)]

    def run(*args):
        first = [pl.BlockSpec(memory_space=pltpu.SMEM)] if smem else specs
        return pl.pallas_call(
            kernel,
            out_shape=outs,
            in_specs=first + specs * (len(args) - 1),
            out_specs=jax.tree.map(lambda _: specs[0], outs),
            scratch_shapes=list(scratch),
            compiler_params=pltpu.CompilerParams(vmem_limit_bytes=56 * 2**20),
            **kw,
        )(*args)

    return run


def shp(*dims, dtype=BF16):
    return jax.ShapeDtypeStruct(dims, dtype)


def body(
    tokens,
    dealing,
    qkv_weight,
    ln1_gain,
    ln1_bias,
    q_bias,
    v_bias,
    out_weight,
    out_bias,
    ln2_gain,
    ln2_bias,
    fc_weight,
    fc_bias,
    proj_weight,
    proj_bias,
    cotangent,
):
    x = lax.axis_index("x")
    c = lax.axis_index("core")
    z = lax.axis_index("z")
    y = lax.axis_index("y")
    deal = dealing[0].reshape(4, 2, 2)
    deal_rel = in_order([deal[0], deal[3], deal[2], deal[1]], rel(0, x))
    deal_rel = jnp.stack([deal_rel[0], deal_rel[3], deal_rel[2], deal_rel[1]])
    deal_own = jnp.where(c == 0, deal_rel[:, 0], deal_rel[:, 1]).reshape(8)
    deal_oth = jnp.where(c == 0, deal_rel[:, 1], deal_rel[:, 0]).reshape(8)
    meta = jnp.concatenate([jnp.stack([x, c, z, y]).astype(jnp.int32), deal_own, deal_oth])

    tok = tokens.reshape(ROWS, D)
    cot = cotangent.reshape(ROWS, D)
    tok_own = gather4(tok, "x")
    tok_oth = [swap(t) for t in tok_own]

    wcols = lax.dynamic_index_in_dim(qkv_weight.reshape(48, 3, 4, CH), x, axis=2, keepdims=False)
    wcols = wcols.reshape(48, 3 * CH)
    row = jnp.concatenate(
        [ln1_gain, ln1_bias, q_bias, v_bias, out_bias, ln2_gain, ln2_bias, proj_bias, fc_bias]
    )
    mine = lax.broadcasted_iota(jnp.int32, (16, 1), 0) == z * 4 + y
    wbuf = jnp.concatenate([wcols, jnp.where(mine, row[None, :], jnp.zeros((), BF16))], axis=0)
    by_z = jnp.concatenate(gather4(wbuf, "z"), axis=0)
    wrel = gather4(by_z, "y")
    rows16 = sum(
        w.reshape(4, 64, 3 * CH)[k, 48:, :].astype(F32) for w in wrel for k in range(4)
    )
    vec = rows16[:, :384].reshape(16, 8, 48).transpose(1, 0, 2).reshape(8, D)
    fcb = rows16[:, 384:].reshape(1, FF)
    qvb = lax.dynamic_index_in_dim(vec[2:4].reshape(2, 4, CH), x, axis=1, keepdims=False)
    qvb = jnp.concatenate([qvb, jnp.zeros((6, CH), F32)], axis=0)

    shard = jnp.concatenate(
        [out_weight, jnp.zeros((16, D), BF16), fc_weight, proj_weight], axis=0
    )
    part = lax.dynamic_slice_in_dim(shard, (x * 2 + c) * 56, 56, axis=0)
    wall = lax.all_gather(part, ("z", "y", "x", "core"), axis=0, tiled=True).reshape(16, 448, D)
    wout = wall[:, :48].reshape(D, D)

    fwd = call(
        forward_kernel,
        [shp(ROWS, CH)] * 4
        + [
            shp(8, HC, HD, BT, dtype=F32),
            shp(8, 8, BT, dtype=F32),
            shp(HC, 1024, HD),
            shp(HC, SEQ, HD),
            shp(HC, HD, SEQ),
            shp(HC, SEQ, HD),
            shp(1024, D),
            shp(D, 3 * CH),
        ],
        [pltpu.VMEM((HC, HD, SEQ), BF16)],
        name="attention_forward",
    )(meta, *tok_own, *tok_oth, *wrel, vec, qvb)
    att, (attt, lse, q, kk, kt, v, normed, w) = fwd[:4], fwd[4:]
    att_rel = [att[0]] + [shift(att[k], "x", -k) for k in (1, 2, 3)]

    whole = lambda *dims: pl.BlockSpec(dims, lambda j: (0,) * len(dims))
    mlp_outs = (
        [shp(ROWS, D), shp(ROWS, D, dtype=F32)]
        + [shp(ROWS, CH)] * 4
        + [shp(4, 4, 112, D)] * 4
        + [shp(8, D, dtype=F32), shp(1, FF, dtype=F32)]
    )
    mlp = pl.pallas_call(
        mlp_kernel,
        grid=(4,),
        out_shape=mlp_outs,
        in_specs=[pl.BlockSpec(memory_space=pltpu.SMEM)]
        + [whole(ROWS, CH)] * 4
        + [whole(ROWS, D), whole(ROWS, D), whole(D, D), whole(8, D), whole(1, FF)]
        + [pl.BlockSpec((4, 448, D), lambda j: (j, 0, 0))],
        out_specs=[whole(*o.shape) for o in mlp_outs],
        scratch_shapes=[
            pltpu.VMEM((ROWS, D), F32),
            pltpu.VMEM((ROWS, D), F32),
            pltpu.VMEM((ROWS, 1), F32),
            pltpu.VMEM((ROWS, D), BF16),
            pltpu.VMEM((ROWS, D), F32),
            pltpu.VMEM((ROWS, D), F32),
            pltpu.VMEM((D, D), BF16),
        ],
        compiler_params=pltpu.CompilerParams(vmem_limit_bytes=56 * 2**20),
        name="feed_forward",
    )(meta, *att_rel, tok, cot, wout, vec, fcb, wall)
    outcome, gm = mlp[0], mlp[1]
    datt, (own_a, own_b, oth_a, oth_b), (vg2, fcg) = mlp[2:6], mlp[6:10], mlp[10:12]

    datt_rel = [datt[0]] + [shift(datt[k], "x", k) for k in (1, 2, 3)]
    recv_a, recv_b = swap(oth_a), swap(oth_b)

    dq, dkv_own, dkv_oth = call(
        backward_kernel,
        [shp(1024, CH), shp(1024, 2 * CH, dtype=F32), shp(1024, 2 * CH)],
        [
            pltpu.VMEM((HC, SEQ, HD), F32),
            pltpu.VMEM((HC, SEQ, HD), F32),
            pltpu.VMEM((HC, 1024, HD), BF16),
        ],
        name="attention_backward",
    )(meta, *datt_rel, q, kk, kt, v, attt, lse)
    dkv_recv = swap(dkv_oth)

    sum_a = [(own_a[k].astype(F32) + recv_a[k].astype(F32)).astype(BF16) for k in range(4)]
    sum_b = [(own_b[k].astype(F32) + recv_b[k].astype(F32)).astype(BF16) for k in range(4)]
    za = scatter4(sum_a, "z")
    yb = scatter4(sum_b, "y")
    fa = scatter4([za[k] for k in range(4)], "y")
    fb = scatter4([yb[k] for k in range(4)], "z")
    quarters = jnp.concatenate([fa, fb], axis=0).reshape(4, 56, D)
    quarters = lax.dynamic_slice_in_dim(jnp.concatenate([quarters, quarters]), x, 4, axis=0)
    quarter = scatter4([quarters[k] for k in range(4)], "x")
    half = in_order(gather4(quarter, "x"), x).reshape(224, D)
    half_oth = swap(half)
    low = jnp.where(c == 0, half, half_oth).astype(F32)
    high = jnp.where(c == 0, half_oth, half).astype(F32)
    grad_fc_w = jnp.concatenate([low[0:96], low[112:208]], axis=0)
    grad_proj_w = jnp.concatenate([high[0:96], high[112:208]], axis=0)
    grad_out_w = jnp.concatenate([low[96:112], low[208:224], high[96:112]], axis=0)

    ng0, ng1, ng2, ng3, g = call(
        input_grad_kernel,
        [shp(ROWS, D)] * 4 + [shp(1024, 3 * CH)],
        smem=False,
        name="input_grad",
    )(dq, dkv_own, dkv_recv, w)
    ng_rel = [ng0] + [shift(n, "x", -k) for k, n in ((1, ng1), (2, ng2), (3, ng3))]
    wq_own, wq_oth, vg1, qvg = call(
        weight_grad_kernel,
        [
            shp(4, 4, 32, 3 * CH),
            shp(4, 4, 32, 3 * CH),
            shp(8, D, dtype=F32),
            shp(1, 3 * CH, dtype=F32),
        ],
        [pltpu.VMEM((D, 3 * CH), BF16)],
        name="weight_grad",
    )(meta, normed, g, *tok_own, ng0, ng1, ng2, ng3)
    token_grad = call(
        token_grad_kernel, shp(ROWS, D, dtype=F32), smem=False, name="token_grad"
    )(tok, gm, vec, *ng_rel)

    place = lambda part: lax.dynamic_update_slice(jnp.zeros((1, D), F32), part, (0, x * CH))
    vg = jnp.concatenate(
        [vg1[0:2], place(qvg[:, :CH]), place(qvg[:, 2 * CH :]), vg2[0:4]], axis=0
    )
    vrows = jnp.concatenate(
        [vg.reshape(8, 16, 48).transpose(1, 0, 2).reshape(16, 384), fcg.reshape(16, 192)], axis=1
    )
    vrows = vrows + swap(vrows)
    vrows = sum(gather4(vrows, "z"))
    vrows = sum(gather4(vrows, "y"))
    vrow = lax.dynamic_slice_in_dim(vrows, z * 4 + y, 1, axis=0)
    vrow = in_order(gather4(vrow, "x"), x)
    vrow = (vrow[0] + vrow[1] + vrow[2] + vrow[3])[0]

    wq_recv = swap(wq_oth)
    wq = [(wq_own[k].astype(F32) + wq_recv[k].astype(F32)).astype(BF16) for k in range(4)]
    wq = scatter4(wq, "z")
    wq = scatter4([wq[k] for k in range(4)], "y")
    wq_x = in_order(gather4(wq, "x"), x)
    wq_x_oth = swap(wq_x)
    grad_qkv = jnp.concatenate(
        [jnp.where(c == 0, wq_x, wq_x_oth), jnp.where(c == 0, wq_x_oth, wq_x)[:, :16]], axis=1
    )
    grad_qkv = (
        grad_qkv.reshape(4, 48, 3, CH).transpose(1, 2, 0, 3).reshape(48, 3 * D).astype(F32)
    )

    vecs = [vrow[k * 48 : (k + 1) * 48] for k in range(8)]
    return (
        outcome.reshape(tokens.shape),
        token_grad.reshape(tokens.shape),
        grad_qkv,
        vecs[0],
        vecs[1],
        vecs[2],
        vecs[3],
        grad_out_w,
        vecs[4],
        vecs[5],
        vecs[6],
        grad_fc_w,
        vrow[384:],
        grad_proj_w,
        vecs[7],
    )


def solution(mesh):
    split = Mesh(mesh.devices.reshape(4, 2, 4, 4), ("x", "core", "z", "y"))
    fsdp = ("z", "y")
    ctx = ("x", "core")
    act = P(fsdp, ctx, None, None)
    mat = P(fsdp, None)
    one = P(fsdp)
    return jax.shard_map(
        body,
        mesh=split,
        in_specs=(act, mat, mat, one, one, one, one, mat, one, one, one, mat, one, mat, one, act),
        out_specs=(act, act, mat, one, one, one, one, mat, one, one, one, mat, one, mat, one),
        check_vma=False,
    )
```

```python
import jax
import jax.numpy as jnp
from jax import lax
from jax.experimental import pallas as pl
from jax.experimental.pallas import tpu as pltpu
from jax.sharding import Mesh, PartitionSpec as P

D = 768
FF = 3072
HC = 3
HD = 64
CH = HC * HD
BT = 128
SEQ = 2048
ROWS = 256
KC = 512
EPS = 1e-05
NEG = -1e30
F32 = jnp.float32
BF16 = jnp.bfloat16

NT = (((1,), (1,)), ((), ()))
TN = (((0,), (0,)), ((), ()))


def dot(a, b):
    return jnp.dot(a, b, preferred_element_type=F32)


def dot_nt(a, b):
    return lax.dot_general(a, b, NT, preferred_element_type=F32)


def dot_tn(a, b):
    return lax.dot_general(a, b, TN, preferred_element_type=F32)


def standardize(v):
    centre = v - jnp.mean(v, axis=-1, keepdims=True)
    spread = jnp.mean(centre * centre, axis=-1, keepdims=True)
    root = lax.rsqrt(spread + EPS)
    return centre * root, root


def rel(a, b):
    return lax.rem(a - b + 4, 4)


def forward_kernel(meta, *refs):
    toks = refs[0:8]
    wrel = refs[8:12]
    vec, qvb = refs[12:14]
    (atts, attt_ref, lse_ref, q_ref, k_ref, kt_ref, v_ref, normed_ref, w_ref) = (
        refs[14:18],
        *refs[18:26],
    )
    vt_ref = refs[26]
    z, y = meta[2], meta[3]
    for ky in range(4):
        for kz in range(4):
            shard = rel(z, kz) * 4 + rel(y, ky)
            w_ref[pl.ds(pl.multiple_of(shard * 48, 16), 48), :] = wrel[ky][kz * 64 : kz * 64 + 48, :]
    gain = vec[0:1, :]
    bias = vec[1:2, :]
    qb = qvb[0:1, :]
    vb = qvb[1:2, :]
    w = w_ref[...]
    for k in range(8):
        own = k < 4
        xhat, _ = standardize(toks[k][...].astype(F32))
        normed = (xhat * gain + bias).astype(BF16)
        if own:
            normed_ref[k * ROWS : (k + 1) * ROWS, :] = normed
            proj = dot(normed, w)
            q = (proj[:, :CH] + qb).astype(BF16) * jnp.asarray(HD**-0.5, BF16)
            for h in range(HC):
                q_ref[h, k * ROWS : (k + 1) * ROWS, :] = q[:, h * HD : (h + 1) * HD]
            kv = proj[:, CH:]
        else:
            kv = dot(normed, w[:, CH:])
        for r in range(2):
            place = pl.multiple_of(meta[4 + 2 * k + r] * BT, BT)
            kk = kv[r * BT : (r + 1) * BT, :CH]
            vv = kv[r * BT : (r + 1) * BT, CH:] + vb
            kb = kk.astype(BF16)
            vbl = vv.astype(BF16)
            for h in range(HC):
                cols = slice(h * HD, (h + 1) * HD)
                k_ref[h, pl.ds(place, BT), :] = kb[:, cols]
                v_ref[h, pl.ds(place, BT), :] = vbl[:, cols]
                kt_ref[h, :, pl.ds(place, BT)] = kk[:, cols].T.astype(BF16)
                vt_ref[h, :, pl.ds(place, BT)] = vv[:, cols].T.astype(BF16)

    key_iota = lax.broadcasted_iota(jnp.int32, (KC, BT), 0)
    query_iota = lax.broadcasted_iota(jnp.int32, (KC, BT), 1)
    for i in range(8):
        pos = meta[4 + i]
        queries = [q_ref[h, i * BT : (i + 1) * BT, :] for h in range(HC)]

        def step(j, carry, masked, pos=pos, queries=queries):
            base = pl.multiple_of(j * KC, KC)
            out = []
            if masked:
                keep = key_iota + base <= query_iota + pos * BT
            for h in range(HC):
                m, total, acc = carry[h]
                s = dot_nt(k_ref[h, pl.ds(base, KC), :], queries[h])
                if masked:
                    s = jnp.where(keep, s, NEG)
                m_new = jnp.maximum(m, jnp.max(s, axis=0, keepdims=True))
                e = jnp.exp(s - m_new)
                a = jnp.exp(m - m_new)
                total = total * a + jnp.sum(e, axis=0, keepdims=True)
                acc = acc * a + dot(vt_ref[h, :, pl.ds(base, KC)], e.astype(BF16))
                out.append((m_new, total, acc))
            return tuple(out)

        full = lax.div(pos * BT, KC)
        carry = tuple(
            (jnp.full((1, BT), NEG, F32), jnp.zeros((1, BT), F32), jnp.zeros((HD, BT), F32))
            for _ in range(HC)
        )
        carry = lax.fori_loop(0, full, lambda j, c: step(j, c, False), carry)
        carry = step(full, carry, True)
        parts = []
        for h in range(HC):
            m, total, acc = carry[h]
            att = acc / total
            attt_ref[i, h] = att
            lse_ref[i, h : h + 1, :] = m + jnp.log(total)
            parts.append(att.T.astype(BF16))
        for h in range(HC):
            atts[i // 2][(i % 2) * BT : (i % 2 + 1) * BT, h * HD : (h + 1) * HD] = parts[h]


def gelu_parts(v):
    c = 0.7978845608028654
    t = jnp.tanh(c * (v + 0.044715 * (v * v * v)))
    act = 0.5 * v * (1.0 + t)
    slope = 0.5 * (1.0 + t) + (0.5 * c) * v * (1.0 - t * t) * (1.0 + (3 * 0.044715) * v * v)
    return act, slope


def head_rows(x, k):
    return pl.ds(pl.multiple_of(lax.rem(x + k, 4) * CH, 64), CH)


def middle_kernel(meta, a0, a1, a2, a3, tok, wout, vec, middle_ref, xhat_ref, root_ref, n2_ref):
    middle = tok[...].astype(F32)
    for k, a in enumerate((a0, a1, a2, a3)):
        middle = middle + dot(a[...], wout[head_rows(meta[0], k), :])
    middle = middle + vec[4:5, :]
    xhat, root = standardize(middle)
    middle_ref[...] = middle
    xhat_ref[...] = xhat
    root_ref[...] = root
    n2_ref[...] = (xhat * vec[5:6, :] + vec[6:7, :]).astype(BF16)


def mlp_kernel(
    n2_own, n2_oth, cot_own, cot_oth, fcb, wblk, ffn_own, ffn_oth, dn_own, dn_oth, dw_ref, fcg_ref, ffn_s, dn_s
):
    j = pl.program_id(0)
    fc = wblk[:, 0:96, :].reshape(D, D)
    proj = wblk[:, 96:192, :].reshape(D, D)
    n2 = jnp.concatenate([n2_own[...], n2_oth[...]], axis=0)
    ct = jnp.concatenate([cot_own[...], cot_oth[...]], axis=0)
    act, slope = gelu_parts(dot_nt(n2, fc) + fcb[j])
    act = act.astype(BF16)
    gh = (dot_nt(ct, proj) * slope).astype(BF16)
    ffn = dot(act, proj)
    dn = dot(gh, fc)
    fcg_ref[j] = jnp.sum(gh.astype(F32), axis=0, keepdims=True)
    dw_ref[:, 0:96, :] = dot_tn(gh, n2).astype(BF16).reshape(8, 96, D)
    dw_ref[:, 96:192, :] = dot_tn(act, ct).astype(BF16).reshape(8, 96, D)

    @pl.when(j == 0)
    def _():
        ffn_s[...] = ffn
        dn_s[...] = dn

    @pl.when(j == 1)
    def _():
        ffn_own[...] = ffn_s[:ROWS] + ffn[:ROWS]
        ffn_oth[...] = (ffn_s[ROWS:] + ffn[ROWS:]).astype(BF16)
        dn_own[...] = dn_s[:ROWS] + dn[:ROWS]
        dn_oth[...] = (dn_s[ROWS:] + dn[ROWS:]).astype(BF16)


def middle_grad_kernel(
    meta,
    dw_in,
    a0,
    a1,
    a2,
    a3,
    cot,
    wout,
    vec,
    xhat_ref,
    root_ref,
    dn_own,
    dn_recv,
    gm_ref,
    d0,
    d1,
    d2,
    d3,
    vg_ref,
    dw_out,
    dout_s,
    sem,
):
    x = meta[0]
    ctf = cot[...].astype(F32)
    dn = dn_own[...] + dn_recv[...].astype(F32)
    xhat = xhat_ref[...]
    e = dn * vec[5:6, :]
    part = e - jnp.mean(e, axis=-1, keepdims=True)
    part = part - xhat * jnp.mean(e * xhat, axis=-1, keepdims=True)
    gm = ctf + part * root_ref[...]
    gm_ref[...] = gm
    gb = gm.astype(BF16)
    for k, (a, d) in enumerate(zip((a0, a1, a2, a3), (d0, d1, d2, d3))):
        d[...] = dot_nt(gb, wout[head_rows(x, k), :]).astype(BF16)
        g = dot_tn(a[...], gb).astype(BF16)
        first = lax.rem(x + k, 4) * 4
        for t in range(4):
            dout_s[first + t] = g[t * 48 : (t + 1) * 48, :]
    copy = pltpu.make_async_copy(dout_s, dw_out.at[:, 192:240, :], sem)
    copy.start()
    vg_ref[...] = jnp.concatenate(
        [
            jnp.sum(gb.astype(F32), axis=0, keepdims=True),
            jnp.sum(dn * xhat, axis=0, keepdims=True),
            jnp.sum(dn, axis=0, keepdims=True),
            jnp.sum(ctf, axis=0, keepdims=True),
            jnp.zeros((4, D), F32),
        ],
        axis=0,
    )
    copy.wait()


def backward_kernel(meta, *refs):
    dos = refs[0:4]
    q_ref, k_ref, kt_ref, v_ref, attt_ref, lse_ref = refs[4:10]
    dq_ref, own_ref, oth_ref = refs[10:13]
    dk_s, dv_s, do_s = refs[13:16]
    dk_s[...] = jnp.zeros_like(dk_s)
    dv_s[...] = jnp.zeros_like(dv_s)
    for k in range(4):
        do = dos[k][...]
        for h in range(HC):
            do_s[h, k * ROWS : (k + 1) * ROWS, :] = do[:, h * HD : (h + 1) * HD]
    key_iota = lax.broadcasted_iota(jnp.int32, (KC, BT), 0)
    query_iota = lax.broadcasted_iota(jnp.int32, (KC, BT), 1)
    for i in range(8):
        pos = meta[4 + i]
        queries = [q_ref[h, i * BT : (i + 1) * BT, :] for h in range(HC)]
        grads = [do_s[h, i * BT : (i + 1) * BT, :] for h in range(HC)]
        lses = [lse_ref[i, h : h + 1, :] for h in range(HC)]
        corrs = [
            jnp.sum(grads[h].astype(F32).T * attt_ref[i, h], axis=0, keepdims=True)
            for h in range(HC)
        ]

        def step(j, carry, masked, pos=pos, queries=queries, grads=grads, lses=lses, corrs=corrs):
            base = pl.multiple_of(j * KC, KC)
            keys = pl.ds(base, KC)
            if masked:
                keep = key_iota + base <= query_iota + pos * BT
            out = []
            for h in range(HC):
                s = dot_nt(k_ref[h, keys, :], queries[h])
                p = jnp.exp(s - lses[h])
                if masked:
                    p = jnp.where(keep, p, 0.0)
                dp = dot_nt(v_ref[h, keys, :], grads[h])
                ds = (p * (dp - corrs[h])).astype(BF16)
                dv_s[h, keys, :] += dot(p.astype(BF16), grads[h])
                dk_s[h, keys, :] += dot(ds, queries[h])
                out.append(carry[h] + dot(kt_ref[h, :, keys], ds))
            return tuple(out)

        full = lax.div(pos * BT, KC)
        carry = tuple(jnp.zeros((HD, BT), F32) for _ in range(HC))
        carry = lax.fori_loop(0, full, lambda j, c: step(j, c, False), carry)
        carry = step(full, carry, True)
        for h in range(HC):
            dq_ref[i * BT : (i + 1) * BT, h * HD : (h + 1) * HD] = (
                (carry[h] * HD**-0.5).T.astype(BF16)
            )
    for i in range(8):
        here = pl.ds(pl.multiple_of(meta[4 + i] * BT, BT), BT)
        there = pl.ds(pl.multiple_of(meta[12 + i] * BT, BT), BT)
        rows = slice(i * BT, (i + 1) * BT)
        for h in range(HC):
            own_ref[rows, h * HD : (h + 1) * HD] = dk_s[h, here, :]
            own_ref[rows, CH + h * HD : CH + (h + 1) * HD] = dv_s[h, here, :]
            oth_ref[rows, h * HD : (h + 1) * HD] = dk_s[h, there, :].astype(BF16)
            oth_ref[rows, CH + h * HD : CH + (h + 1) * HD] = dv_s[h, there, :].astype(BF16)


def input_grad_kernel(dq_ref, own_ref, recv_ref, w_ref, n0, n1, n2, n3, g_ref):
    g_ref[:, :CH] = dq_ref[...]
    g_ref[:, CH:] = (own_ref[...] + recv_ref[...].astype(F32)).astype(BF16)
    w = w_ref[...]
    for k, n in enumerate((n0, n1, n2, n3)):
        n[...] = dot_nt(g_ref[k * ROWS : (k + 1) * ROWS, :], w).astype(BF16)


def weight_grad_kernel(
    meta, normed_ref, g_ref, t0, t1, t2, t3, n0, n1, n2, n3, vg2, fcg, own_ref, oth_ref, dw_s, vec_s, row_s
):
    x, c, z, y = meta[0], meta[1], meta[2], meta[3]
    g = g_ref[...]
    dw_s[...] = dot_tn(normed_ref[...], g).astype(BF16)
    gain = jnp.zeros((1, D), F32)
    bias = jnp.zeros((1, D), F32)
    for t, n in zip((t0, t1, t2, t3), (n0, n1, n2, n3)):
        xhat, _ = standardize(t[...].astype(F32))
        ng = n[...].astype(F32)
        gain = gain + jnp.sum(ng * xhat, axis=0, keepdims=True)
        bias = bias + jnp.sum(ng, axis=0, keepdims=True)
    sums = jnp.sum(g.astype(F32), axis=0, keepdims=True)
    vec_s[0:1, :] = gain
    vec_s[1:2, :] = bias
    vec_s[2:4, :] = jnp.zeros((2, D), F32)
    for i in range(4):

        @pl.when(x == i)
        def _():
            vec_s[2:3, i * CH : (i + 1) * CH] = sums[:, :CH]
            vec_s[3:4, i * CH : (i + 1) * CH] = sums[:, 2 * CH :]

    vec_s[4:8, :] = vg2[0:4, :]
    row_s[...] = jnp.zeros_like(row_s)
    for s in range(16):
        for v in range(8):
            row_s[s, 0:1, v * 48 : (v + 1) * 48] = vec_s[v : v + 1, s * 48 : (s + 1) * 48]

        @pl.when(c == 0)
        def _():
            row_s[s, 0:1, 384:480] = fcg[s // 8, :, (s % 8) * 96 : (s % 8 + 1) * 96]

        @pl.when(c == 1)
        def _():
            row_s[s, 0:1, 480:576] = fcg[s // 8, :, (s % 8) * 96 : (s % 8 + 1) * 96]

    blank = jnp.zeros((16, HC * CH), BF16)
    for s in range(16):
        sz, sy = rel(s // 4, z), rel(s % 4, y)
        first = dw_s[s * 48 : s * 48 + 32, :]
        second = dw_s[s * 48 + 32 : s * 48 + 48, :]
        row = row_s[s].astype(BF16)
        own_ref[sz, sy, 32:48, :] = row
        oth_ref[sz, sy, 32:48, :] = row

        @pl.when(c == 0)
        def _():
            own_ref[sz, sy, 0:32, :] = first
            oth_ref[sz, sy, 0:16, :] = second
            oth_ref[sz, sy, 16:32, :] = blank

        @pl.when(c == 1)
        def _():
            oth_ref[sz, sy, 0:32, :] = first
            own_ref[sz, sy, 0:16, :] = second
            own_ref[sz, sy, 16:32, :] = blank


def token_grad_kernel(tok, gm, vec, n0, n1, n2, n3, out_ref):
    ng = n0[...].astype(F32) + n1[...].astype(F32) + n2[...].astype(F32) + n3[...].astype(F32)
    xhat, root = standardize(tok[...].astype(F32))
    e = ng * vec[0:1, :]
    part = e - jnp.mean(e, axis=-1, keepdims=True)
    part = part - xhat * jnp.mean(e * xhat, axis=-1, keepdims=True)
    out_ref[...] = gm[...] + part * root


def shift(v, axis, k):
    return lax.ppermute(v, axis, [(i, (i + k) % 4) for i in range(4)])


def swap(v):
    return lax.ppermute(v, "core", [(0, 1), (1, 0)])


def gather4(v, axis):
    return [v] + [shift(v, axis, k) for k in (1, 2, 3)]


def scatter4(pieces, axis):
    total = pieces[0].astype(F32)
    for k in (1, 2, 3):
        total = total + shift(pieces[k], axis, k).astype(F32)
    return total.astype(BF16)


def sum4(pieces):
    return (pieces[0] + pieces[2]) + (pieces[1] + pieces[3])


def in_order(pieces, index):
    up = [pieces[0], pieces[3], pieces[2], pieces[1]]
    twice = jnp.stack(up + up)
    return lax.dynamic_slice_in_dim(twice, rel(0, index), 4, axis=0)


def call(kernel, outs, scratch=(), smem=True, us=0, **kw):
    specs = [pl.BlockSpec(memory_space=pltpu.VMEM)]

    def run(*args):
        first = [pl.BlockSpec(memory_space=pltpu.SMEM)] if smem else specs
        return pl.pallas_call(
            kernel,
            out_shape=outs,
            in_specs=first + specs * (len(args) - 1),
            out_specs=jax.tree.map(lambda _: specs[0], outs),
            scratch_shapes=list(scratch),
            compiler_params=pltpu.CompilerParams(vmem_limit_bytes=56 * 2**20),
            cost_estimate=cost(us),
            **kw,
        )(*args)

    return run


def cost(us):
    return pl.CostEstimate(flops=us * 10**9, bytes_accessed=us * 10**6, transcendentals=0)


def shp(*dims, dtype=BF16):
    return jax.ShapeDtypeStruct(dims, dtype)


def body(
    tokens,
    dealing,
    qkv_weight,
    ln1_gain,
    ln1_bias,
    q_bias,
    v_bias,
    out_weight,
    out_bias,
    ln2_gain,
    ln2_bias,
    fc_weight,
    fc_bias,
    proj_weight,
    proj_bias,
    cotangent,
):
    x = lax.axis_index("x")
    c = lax.axis_index("core")
    z = lax.axis_index("z")
    y = lax.axis_index("y")
    deal = dealing[0].reshape(4, 2, 2)
    deal_rel = in_order([deal[0], deal[3], deal[2], deal[1]], rel(0, x))
    deal_rel = jnp.stack([deal_rel[0], deal_rel[3], deal_rel[2], deal_rel[1]])
    deal_own = jnp.where(c == 0, deal_rel[:, 0], deal_rel[:, 1]).reshape(8)
    deal_oth = jnp.where(c == 0, deal_rel[:, 1], deal_rel[:, 0]).reshape(8)
    meta = jnp.concatenate([jnp.stack([x, c, z, y]).astype(jnp.int32), deal_own, deal_oth])

    tok = tokens.reshape(ROWS, D)
    cot = cotangent.reshape(ROWS, D)
    wcols = lax.dynamic_index_in_dim(qkv_weight.reshape(48, 3, 4, CH), x, axis=2, keepdims=False)
    wcols = wcols.reshape(48, 3 * CH)
    row = jnp.concatenate(
        [ln1_gain, ln1_bias, q_bias, v_bias, out_bias, ln2_gain, ln2_bias, proj_bias, fc_bias]
    )
    mine = lax.broadcasted_iota(jnp.int32, (16, 1), 0) == z * 4 + y
    wbuf = jnp.concatenate([wcols, jnp.where(mine, row[None, :], jnp.zeros((), BF16))], axis=0)
    by_z = jnp.concatenate(gather4(wbuf, "z"), axis=0)
    by_z, tok_1, tok_3 = lax.optimization_barrier((by_z, shift(tok, "x", 1), shift(tok, "x", 3)))
    tok_far, _ = lax.optimization_barrier((tok, by_z))
    tok_own = [tok, tok_1, shift(tok_far, "x", 2), tok_3]
    tok_oth = [swap(t) for t in tok_own]
    wrel = gather4(by_z, "y")
    rows16 = sum(
        w.reshape(4, 64, 3 * CH)[k, 48:, :].astype(F32) for w in wrel for k in range(4)
    )
    vec = rows16[:, :384].reshape(16, 8, 48).transpose(1, 0, 2).reshape(8, D)
    fcb = rows16[:, 384:].reshape(1, FF)
    qvb = lax.dynamic_index_in_dim(vec[2:4].reshape(2, 4, CH), x, axis=1, keepdims=False)
    qvb = jnp.concatenate([qvb, jnp.zeros((6, CH), F32)], axis=0)

    half = lambda w, n: lax.dynamic_slice_in_dim(w, c * n, n, axis=0)
    part = jnp.concatenate(
        [half(fc_weight, 96), half(proj_weight, 96), half(out_weight, 24), jnp.zeros((8, D), BF16)],
        axis=0,
    )
    wall = lax.all_gather(part, ("z", "y"), axis=0, tiled=True).reshape(16, 224, D)
    fcb = lax.dynamic_index_in_dim(fcb.reshape(16, 2, 96), c, axis=1, keepdims=False)
    fcb = fcb.reshape(2, 1, D)
    cot_oth = swap(cot)

    fwd = call(
        forward_kernel,
        [shp(ROWS, CH)] * 4
        + [
            shp(8, HC, HD, BT, dtype=F32),
            shp(8, 8, BT, dtype=F32),
            shp(HC, 1024, HD),
            shp(HC, SEQ, HD),
            shp(HC, HD, SEQ),
            shp(HC, SEQ, HD),
            shp(1024, D),
            shp(D, 3 * CH),
        ],
        [pltpu.VMEM((HC, HD, SEQ), BF16)],
        us=25,
        name="attention_forward",
    )(meta, *tok_own, *tok_oth, *wrel, vec, qvb)
    att, (attt, lse, q, kk, kt, v, normed, w) = fwd[:4], fwd[4:]
    wall, first = lax.optimization_barrier((wall, att[0]))
    att = [first, *att[1:]]
    out_half = wall[:, 192:216]
    out_recv = swap(out_half)
    wout = jnp.stack(
        [jnp.where(c == 0, out_half, out_recv), jnp.where(c == 0, out_recv, out_half)], axis=1
    ).reshape(D, D)
    att_rel = [att[0]] + [shift(att[k], "x", -k) for k in (1, 2, 3)]

    middle, xhat, root, n2 = call(
        middle_kernel,
        [shp(ROWS, D, dtype=F32), shp(ROWS, D, dtype=F32), shp(ROWS, 1, dtype=F32), shp(ROWS, D)],
        us=4,
        name="middle",
    )(meta, *att_rel, tok, wout, vec)
    n2_oth = swap(n2)

    whole = lambda *dims: pl.BlockSpec(dims, lambda j: (0,) * len(dims))
    mlp_outs = [
        shp(ROWS, D, dtype=F32),
        shp(ROWS, D),
        shp(ROWS, D, dtype=F32),
        shp(ROWS, D),
        shp(16, 240, D),
        shp(2, 1, D, dtype=F32),
    ]
    mlp_specs = [whole(*o.shape) for o in mlp_outs]
    mlp_specs[4] = pl.BlockSpec((8, 240, D), lambda j: (j, 0, 0))
    ffn_own, ffn_oth, dn_own, dn_oth, dw, fcg = pl.pallas_call(
        mlp_kernel,
        grid=(2,),
        out_shape=mlp_outs,
        in_specs=[whole(ROWS, D)] * 4
        + [whole(2, 1, D), pl.BlockSpec((8, 224, D), lambda j: (j, 0, 0))],
        out_specs=mlp_specs,
        scratch_shapes=[pltpu.VMEM((2 * ROWS, D), F32), pltpu.VMEM((2 * ROWS, D), F32)],
        compiler_params=pltpu.CompilerParams(vmem_limit_bytes=56 * 2**20),
        cost_estimate=cost(18),
        name="feed_forward",
    )(n2, n2_oth, cot, cot_oth, fcb, wall)
    dn_recv = swap(dn_oth)
    ffn_recv = swap(ffn_oth)
    outcome = (middle + (ffn_own + ffn_recv.astype(F32)) + vec[7:8]).astype(BF16)

    vmem = pl.BlockSpec(memory_space=pltpu.VMEM)
    hbm = pl.BlockSpec(memory_space=pl.ANY)
    gm, *datt, vg2, dw = pl.pallas_call(
        middle_grad_kernel,
        out_shape=[shp(ROWS, D, dtype=F32)]
        + [shp(ROWS, CH)] * 4
        + [shp(8, D, dtype=F32), shp(16, 240, D)],
        in_specs=[pl.BlockSpec(memory_space=pltpu.SMEM), hbm] + [vmem] * 11,
        out_specs=[vmem] * 6 + [hbm],
        scratch_shapes=[pltpu.VMEM((16, 48, D), BF16), pltpu.SemaphoreType.DMA],
        input_output_aliases={1: 6},
        compiler_params=pltpu.CompilerParams(vmem_limit_bytes=56 * 2**20),
        cost_estimate=cost(5),
        name="middle_grad",
    )(meta, dw, *att_rel, cot, wout, vec, xhat, root, dn_own, dn_recv)
    shard_grad = lax.psum_scatter(
        dw.reshape(16 * 240, D), ("z", "y"), scatter_dimension=0, tiled=True
    )

    datt_rel = [datt[0]] + [shift(datt[k], "x", k) for k in (1, 2, 3)]
    dq, dkv_own, dkv_oth = call(
        backward_kernel,
        [shp(1024, CH), shp(1024, 2 * CH, dtype=F32), shp(1024, 2 * CH)],
        [
            pltpu.VMEM((HC, SEQ, HD), F32),
            pltpu.VMEM((HC, SEQ, HD), F32),
            pltpu.VMEM((HC, 1024, HD), BF16),
        ],
        us=24,
        name="attention_backward",
    )(meta, *datt_rel, q, kk, kt, v, attt, lse)
    dkv_recv = swap(dkv_oth)

    ng0, ng1, ng2, ng3, g = call(
        input_grad_kernel,
        [shp(ROWS, D)] * 4 + [shp(1024, 3 * CH)],
        smem=False,
        us=5,
        name="input_grad",
    )(dq, dkv_own, dkv_recv, w)
    ng_rel = [ng0] + [shift(n, "x", -k) for k, n in ((1, ng1), (2, ng2), (3, ng3))]
    wq_own, wq_oth = call(
        weight_grad_kernel,
        [shp(4, 4, 48, 3 * CH)] * 2,
        [
            pltpu.VMEM((D, 3 * CH), BF16),
            pltpu.VMEM((8, D), F32),
            pltpu.VMEM((16, 16, 3 * CH), F32),
        ],
        us=8,
        name="weight_grad",
    )(meta, normed, g, *tok_own, ng0, ng1, ng2, ng3, vg2, fcg)
    token_grad = call(
        token_grad_kernel, shp(ROWS, D, dtype=F32), smem=False, us=3, name="token_grad"
    )(tok, gm, vec, *ng_rel)

    wq_recv = swap(wq_oth)
    wq = [(wq_own[k].astype(F32) + wq_recv[k].astype(F32)).astype(BF16) for k in range(4)]
    wq = scatter4(wq, "z")
    wq, token_grad = lax.optimization_barrier((wq, token_grad))
    wq = scatter4([wq[k] for k in range(4)], "y")
    wq_rel = gather4(wq, "x")
    vrow = sum4([w[32].astype(F32) for w in wq_rel])
    wq_x = in_order(wq_rel, x)[:, :32]
    wq_x_oth = swap(wq_x)
    grad_qkv = jnp.concatenate(
        [jnp.where(c == 0, wq_x, wq_x_oth), jnp.where(c == 0, wq_x_oth, wq_x)[:, :16]], axis=1
    )
    grad_qkv = (
        grad_qkv.reshape(4, 48, 3, CH).transpose(1, 2, 0, 3).reshape(48, 3 * D).astype(F32)
    )

    shard_grad = sum4([v.astype(F32) for v in gather4(shard_grad, "x")]).astype(BF16)
    shard_oth = swap(shard_grad).astype(F32)
    shard_grad = shard_grad.astype(F32)
    low = jnp.where(c == 0, shard_grad, shard_oth)
    high = jnp.where(c == 0, shard_oth, shard_grad)
    grad_fc_w = jnp.concatenate([low[0:96], high[0:96]], axis=0)
    grad_proj_w = jnp.concatenate([low[96:192], high[96:192]], axis=0)
    grad_out_w = shard_grad[192:] + shard_oth[192:]

    vecs = [vrow[k * 48 : (k + 1) * 48] for k in range(8)]
    return (
        outcome.reshape(tokens.shape),
        token_grad.reshape(tokens.shape),
        grad_qkv,
        vecs[0],
        vecs[1],
        vecs[2],
        vecs[3],
        grad_out_w,
        vecs[4],
        vecs[5],
        vecs[6],
        grad_fc_w,
        vrow[384:],
        grad_proj_w,
        vecs[7],
    )


def solution(mesh):
    split = Mesh(mesh.devices.reshape(4, 2, 4, 4), ("x", "core", "z", "y"))
    fsdp = ("z", "y")
    ctx = ("x", "core")
    act = P(fsdp, ctx, None, None)
    mat = P(fsdp, None)
    one = P(fsdp)
    return jax.shard_map(
        body,
        mesh=split,
        in_specs=(act, mat, mat, one, one, one, one, mat, one, one, one, mat, one, mat, one, act),
        out_specs=(act, act, mat, one, one, one, one, mat, one, one, one, mat, one, mat, one),
        check_vma=False,
    )
```

```python
import jax
import jax.numpy as jnp
from jax import lax
from jax.experimental import pallas as pl
from jax.experimental.pallas import tpu as pltpu
from jax.sharding import Mesh, PartitionSpec as P

D = 768
FF = 3072
HC = 3
HD = 64
CH = HC * HD
BT = 128
SEQ = 2048
ROWS = 256
KC = 512
EPS = 1e-05
NEG = -1e30
F32 = jnp.float32
BF16 = jnp.bfloat16

NT = (((1,), (1,)), ((), ()))
TN = (((0,), (0,)), ((), ()))


def dot(a, b):
    return jnp.dot(a, b, preferred_element_type=F32)


def dot_nt(a, b):
    return lax.dot_general(a, b, NT, preferred_element_type=F32)


def dot_tn(a, b):
    return lax.dot_general(a, b, TN, preferred_element_type=F32)


def standardize(v):
    centre = v - jnp.mean(v, axis=-1, keepdims=True)
    spread = jnp.mean(centre * centre, axis=-1, keepdims=True)
    root = lax.rsqrt(spread + EPS)
    return centre * root, root


def rel(a, b):
    return lax.rem(a - b + 4, 4)


def forward_kernel(meta, *refs):
    toks = refs[0:8]
    wall, vec, qvb = refs[8:11]
    (atts, attt_ref, lse_ref, q_ref, k_ref, kt_ref, v_ref, normed_ref, w_ref) = (
        refs[11:15],
        *refs[15:23],
    )
    vt_ref = refs[23]
    for s in range(16):
        w_ref[s * 48 : (s + 1) * 48, :] = wall[s, 0:48, :]
    gain = vec[0:1, :]
    bias = vec[1:2, :]
    qb = qvb[0:1, :]
    vb = qvb[1:2, :]
    w = w_ref[...]
    for k in range(8):
        own = k < 4
        xhat, _ = standardize(toks[k][...].astype(F32))
        normed = (xhat * gain + bias).astype(BF16)
        if own:
            normed_ref[k * ROWS : (k + 1) * ROWS, :] = normed
            proj = dot(normed, w)
            q = (proj[:, :CH] + qb).astype(BF16) * jnp.asarray(HD**-0.5, BF16)
            for h in range(HC):
                q_ref[h, k * ROWS : (k + 1) * ROWS, :] = q[:, h * HD : (h + 1) * HD]
            kv = proj[:, CH:]
        else:
            kv = dot(normed, w[:, CH:])
        for r in range(2):
            place = pl.multiple_of(meta[4 + 2 * k + r] * BT, BT)
            kk = kv[r * BT : (r + 1) * BT, :CH]
            vv = kv[r * BT : (r + 1) * BT, CH:] + vb
            kb = kk.astype(BF16)
            vbl = vv.astype(BF16)
            for h in range(HC):
                cols = slice(h * HD, (h + 1) * HD)
                k_ref[h, pl.ds(place, BT), :] = kb[:, cols]
                v_ref[h, pl.ds(place, BT), :] = vbl[:, cols]
                kt_ref[h, :, pl.ds(place, BT)] = kk[:, cols].T.astype(BF16)
                vt_ref[h, :, pl.ds(place, BT)] = vv[:, cols].T.astype(BF16)

    key_iota = lax.broadcasted_iota(jnp.int32, (KC, BT), 0)
    query_iota = lax.broadcasted_iota(jnp.int32, (KC, BT), 1)
    for i in range(8):
        pos = meta[4 + i]
        queries = [q_ref[h, i * BT : (i + 1) * BT, :] for h in range(HC)]

        def step(j, carry, masked, pos=pos, queries=queries):
            base = pl.multiple_of(j * KC, KC)
            out = []
            if masked:
                keep = key_iota + base <= query_iota + pos * BT
            for h in range(HC):
                m, total, acc = carry[h]
                s = dot_nt(k_ref[h, pl.ds(base, KC), :], queries[h])
                if masked:
                    s = jnp.where(keep, s, NEG)
                m_new = jnp.maximum(m, jnp.max(s, axis=0, keepdims=True))
                e = jnp.exp(s - m_new)
                a = jnp.exp(m - m_new)
                total = total * a + jnp.sum(e, axis=0, keepdims=True)
                acc = acc * a + dot(vt_ref[h, :, pl.ds(base, KC)], e.astype(BF16))
                out.append((m_new, total, acc))
            return tuple(out)

        full = lax.div(pos * BT, KC)
        carry = tuple(
            (jnp.full((1, BT), NEG, F32), jnp.zeros((1, BT), F32), jnp.zeros((HD, BT), F32))
            for _ in range(HC)
        )
        carry = lax.fori_loop(0, full, lambda j, c: step(j, c, False), carry)
        carry = step(full, carry, True)
        parts = []
        for h in range(HC):
            m, total, acc = carry[h]
            att = acc / total
            attt_ref[i, h] = att
            lse_ref[i, h : h + 1, :] = m + jnp.log(total)
            parts.append(att.T.astype(BF16))
        for h in range(HC):
            atts[i // 2][(i % 2) * BT : (i % 2 + 1) * BT, h * HD : (h + 1) * HD] = parts[h]


def gelu_parts(v):
    c = 0.7978845608028654
    t = jnp.tanh(c * (v + 0.044715 * (v * v * v)))
    act = 0.5 * v * (1.0 + t)
    slope = 0.5 * (1.0 + t) + (0.5 * c) * v * (1.0 - t * t) * (1.0 + (3 * 0.044715) * v * v)
    return act, slope


def head_rows(wout, x, k):
    return wout[pl.ds(lax.rem(x + k, 4) * 4, 4)].reshape(CH, D)


def middle_kernel(meta, a0, a1, a2, a3, tok, wout, vec, middle_ref, xhat_ref, root_ref, n2_ref):
    middle = tok[...].astype(F32)
    for k, a in enumerate((a0, a1, a2, a3)):
        middle = middle + dot(a[...], head_rows(wout, meta[0], k))
    middle = middle + vec[4:5, :]
    xhat, root = standardize(middle)
    middle_ref[...] = middle
    xhat_ref[...] = xhat
    root_ref[...] = root
    n2_ref[...] = (xhat * vec[5:6, :] + vec[6:7, :]).astype(BF16)


def mlp_kernel(
    n2_own, n2_oth, cot_own, cot_oth, fcb, wblk, ffn_own, ffn_oth, dn_own, dn_oth, dw_ref, fcg_ref, ffn_s, dn_s
):
    j = pl.program_id(0)
    fc = wblk[:, 0:96, :].reshape(D, D)
    proj = wblk[:, 96:192, :].reshape(D, D)
    n2 = jnp.concatenate([n2_own[...], n2_oth[...]], axis=0)
    ct = jnp.concatenate([cot_own[...], cot_oth[...]], axis=0)
    act, slope = gelu_parts(dot_nt(n2, fc) + fcb[j])
    act = act.astype(BF16)
    gh = (dot_nt(ct, proj) * slope).astype(BF16)
    ffn = dot(act, proj)
    dn = dot(gh, fc)
    fcg_ref[j] = jnp.sum(gh.astype(F32), axis=0, keepdims=True)
    dw_ref[:, 0:96, :] = dot_tn(gh, n2).astype(BF16).reshape(8, 96, D)
    dw_ref[:, 96:192, :] = dot_tn(act, ct).astype(BF16).reshape(8, 96, D)

    @pl.when(j == 0)
    def _():
        ffn_s[...] = ffn
        dn_s[...] = dn

    @pl.when(j == 1)
    def _():
        ffn_own[...] = ffn_s[:ROWS] + ffn[:ROWS]
        ffn_oth[...] = (ffn_s[ROWS:] + ffn[ROWS:]).astype(BF16)
        dn_own[...] = dn_s[:ROWS] + dn[:ROWS]
        dn_oth[...] = (dn_s[ROWS:] + dn[ROWS:]).astype(BF16)


def middle_grad_kernel(
    meta,
    dw_in,
    a0,
    a1,
    a2,
    a3,
    cot,
    wout,
    vec,
    xhat_ref,
    root_ref,
    dn_own,
    dn_recv,
    gm_ref,
    d0,
    d1,
    d2,
    d3,
    vg_ref,
    dw_out,
    dout_s,
    sem,
):
    x = meta[0]
    ctf = cot[...].astype(F32)
    dn = dn_own[...] + dn_recv[...].astype(F32)
    xhat = xhat_ref[...]
    e = dn * vec[5:6, :]
    part = e - jnp.mean(e, axis=-1, keepdims=True)
    part = part - xhat * jnp.mean(e * xhat, axis=-1, keepdims=True)
    gm = ctf + part * root_ref[...]
    gm_ref[...] = gm
    gb = gm.astype(BF16)
    for k, (a, d) in enumerate(zip((a0, a1, a2, a3), (d0, d1, d2, d3))):
        d[...] = dot_nt(gb, head_rows(wout, x, k)).astype(BF16)
        g = dot_tn(a[...], gb).astype(BF16)
        first = lax.rem(x + k, 4) * 4
        for t in range(4):
            dout_s[first + t] = g[t * 48 : (t + 1) * 48, :]
    copy = pltpu.make_async_copy(dout_s, dw_out.at[:, 192:240, :], sem)
    copy.start()
    vg_ref[...] = jnp.concatenate(
        [
            jnp.sum(gb.astype(F32), axis=0, keepdims=True),
            jnp.sum(dn * xhat, axis=0, keepdims=True),
            jnp.sum(dn, axis=0, keepdims=True),
            jnp.sum(ctf, axis=0, keepdims=True),
            jnp.zeros((4, D), F32),
        ],
        axis=0,
    )
    copy.wait()


def backward_kernel(meta, *refs):
    dos = refs[0:4]
    q_ref, k_ref, kt_ref, v_ref, attt_ref, lse_ref = refs[4:10]
    dq_ref, own_ref, oth_ref = refs[10:13]
    dk_s, dv_s, do_s = refs[13:16]
    dk_s[...] = jnp.zeros_like(dk_s)
    dv_s[...] = jnp.zeros_like(dv_s)
    for k in range(4):
        do = dos[k][...]
        for h in range(HC):
            do_s[h, k * ROWS : (k + 1) * ROWS, :] = do[:, h * HD : (h + 1) * HD]
    key_iota = lax.broadcasted_iota(jnp.int32, (KC, BT), 0)
    query_iota = lax.broadcasted_iota(jnp.int32, (KC, BT), 1)
    for i in range(8):
        pos = meta[4 + i]
        queries = [q_ref[h, i * BT : (i + 1) * BT, :] for h in range(HC)]
        grads = [do_s[h, i * BT : (i + 1) * BT, :] for h in range(HC)]
        lses = [lse_ref[i, h : h + 1, :] for h in range(HC)]
        corrs = [
            jnp.sum(grads[h].astype(F32).T * attt_ref[i, h], axis=0, keepdims=True)
            for h in range(HC)
        ]

        def step(j, carry, masked, pos=pos, queries=queries, grads=grads, lses=lses, corrs=corrs):
            base = pl.multiple_of(j * KC, KC)
            keys = pl.ds(base, KC)
            if masked:
                keep = key_iota + base <= query_iota + pos * BT
            out = []
            for h in range(HC):
                s = dot_nt(k_ref[h, keys, :], queries[h])
                p = jnp.exp(s - lses[h])
                if masked:
                    p = jnp.where(keep, p, 0.0)
                dp = dot_nt(v_ref[h, keys, :], grads[h])
                ds = (p * (dp - corrs[h])).astype(BF16)
                dv_s[h, keys, :] += dot(p.astype(BF16), grads[h])
                dk_s[h, keys, :] += dot(ds, queries[h])
                out.append(carry[h] + dot(kt_ref[h, :, keys], ds))
            return tuple(out)

        full = lax.div(pos * BT, KC)
        carry = tuple(jnp.zeros((HD, BT), F32) for _ in range(HC))
        carry = lax.fori_loop(0, full, lambda j, c: step(j, c, False), carry)
        carry = step(full, carry, True)
        for h in range(HC):
            dq_ref[i * BT : (i + 1) * BT, h * HD : (h + 1) * HD] = (
                (carry[h] * HD**-0.5).T.astype(BF16)
            )
    for i in range(8):
        here = pl.ds(pl.multiple_of(meta[4 + i] * BT, BT), BT)
        there = pl.ds(pl.multiple_of(meta[12 + i] * BT, BT), BT)
        rows = slice(i * BT, (i + 1) * BT)
        for h in range(HC):
            own_ref[rows, h * HD : (h + 1) * HD] = dk_s[h, here, :]
            own_ref[rows, CH + h * HD : CH + (h + 1) * HD] = dv_s[h, here, :]
            oth_ref[rows, h * HD : (h + 1) * HD] = dk_s[h, there, :].astype(BF16)
            oth_ref[rows, CH + h * HD : CH + (h + 1) * HD] = dv_s[h, there, :].astype(BF16)


def input_grad_kernel(dq_ref, own_ref, recv_ref, w_ref, n0, n1, n2, n3, g_ref):
    g_ref[:, :CH] = dq_ref[...]
    g_ref[:, CH:] = (own_ref[...] + recv_ref[...].astype(F32)).astype(BF16)
    w = w_ref[...]
    for k, n in enumerate((n0, n1, n2, n3)):
        n[...] = dot_nt(g_ref[k * ROWS : (k + 1) * ROWS, :], w).astype(BF16)


def weight_grad_kernel(
    meta, normed_ref, g_ref, t0, t1, t2, t3, n0, n1, n2, n3, vg2, fcg, grad_ref, vec_s, row_s
):
    x, c = meta[0], meta[1]
    g = g_ref[...]
    grad_ref[:, 0:48, :] = dot_tn(normed_ref[...], g).astype(BF16).reshape(16, 48, HC * CH)
    gain = jnp.zeros((1, D), F32)
    bias = jnp.zeros((1, D), F32)
    for t, n in zip((t0, t1, t2, t3), (n0, n1, n2, n3)):
        xhat, _ = standardize(t[...].astype(F32))
        ng = n[...].astype(F32)
        gain = gain + jnp.sum(ng * xhat, axis=0, keepdims=True)
        bias = bias + jnp.sum(ng, axis=0, keepdims=True)
    sums = jnp.sum(g.astype(F32), axis=0, keepdims=True)
    vec_s[0:1, :] = gain
    vec_s[1:2, :] = bias
    vec_s[2:4, :] = jnp.zeros((2, D), F32)
    for i in range(4):

        @pl.when(x == i)
        def _():
            vec_s[2:3, i * CH : (i + 1) * CH] = sums[:, :CH]
            vec_s[3:4, i * CH : (i + 1) * CH] = sums[:, 2 * CH :]

    vec_s[4:8, :] = vg2[0:4, :]
    row_s[...] = jnp.zeros_like(row_s)
    for s in range(16):
        for v in range(8):
            row_s[s, 0:1, v * 48 : (v + 1) * 48] = vec_s[v : v + 1, s * 48 : (s + 1) * 48]

        @pl.when(c == 0)
        def _():
            row_s[s, 0:1, 384:480] = fcg[s // 8, :, (s % 8) * 96 : (s % 8 + 1) * 96]

        @pl.when(c == 1)
        def _():
            row_s[s, 0:1, 480:576] = fcg[s // 8, :, (s % 8) * 96 : (s % 8 + 1) * 96]

    for s in range(16):
        grad_ref[s, 48:64, :] = row_s[s].astype(BF16)


def token_grad_kernel(tok, gm, vec, n0, n1, n2, n3, out_ref):
    ng = n0[...].astype(F32) + n1[...].astype(F32) + n2[...].astype(F32) + n3[...].astype(F32)
    xhat, root = standardize(tok[...].astype(F32))
    e = ng * vec[0:1, :]
    part = e - jnp.mean(e, axis=-1, keepdims=True)
    part = part - xhat * jnp.mean(e * xhat, axis=-1, keepdims=True)
    out_ref[...] = gm[...] + part * root


def shift(v, axis, k):
    return lax.ppermute(v, axis, [(i, (i + k) % 4) for i in range(4)])


def swap(v):
    return lax.ppermute(v, "core", [(0, 1), (1, 0)])


def gather4(v, axis):
    return [v] + [shift(v, axis, k) for k in (1, 2, 3)]


def scatter4(pieces, axis):
    total = pieces[0].astype(F32)
    for k in (1, 2, 3):
        total = total + shift(pieces[k], axis, k).astype(F32)
    return total.astype(BF16)


def sum4(pieces):
    return (pieces[0] + pieces[2]) + (pieces[1] + pieces[3])


def in_order(pieces, index):
    up = [pieces[0], pieces[3], pieces[2], pieces[1]]
    twice = jnp.stack(up + up)
    return lax.dynamic_slice_in_dim(twice, rel(0, index), 4, axis=0)


def call(kernel, outs, scratch=(), smem=True, us=0, **kw):
    specs = [pl.BlockSpec(memory_space=pltpu.VMEM)]

    def run(*args):
        first = [pl.BlockSpec(memory_space=pltpu.SMEM)] if smem else specs
        return pl.pallas_call(
            kernel,
            out_shape=outs,
            in_specs=first + specs * (len(args) - 1),
            out_specs=jax.tree.map(lambda _: specs[0], outs),
            scratch_shapes=list(scratch),
            compiler_params=pltpu.CompilerParams(vmem_limit_bytes=56 * 2**20),
            cost_estimate=cost(us),
            **kw,
        )(*args)

    return run


def cost(us):
    return pl.CostEstimate(flops=us * 2 * 10**8, bytes_accessed=us * 2 * 10**5, transcendentals=0)


def shp(*dims, dtype=BF16):
    return jax.ShapeDtypeStruct(dims, dtype)


def body(
    tokens,
    dealing,
    qkv_weight,
    ln1_gain,
    ln1_bias,
    q_bias,
    v_bias,
    out_weight,
    out_bias,
    ln2_gain,
    ln2_bias,
    fc_weight,
    fc_bias,
    proj_weight,
    proj_bias,
    cotangent,
):
    x = lax.axis_index("x")
    c = lax.axis_index("core")
    z = lax.axis_index("z")
    y = lax.axis_index("y")
    deal = dealing[0].reshape(4, 2, 2)
    deal_rel = in_order([deal[0], deal[3], deal[2], deal[1]], rel(0, x))
    deal_rel = jnp.stack([deal_rel[0], deal_rel[3], deal_rel[2], deal_rel[1]])
    deal_own = jnp.where(c == 0, deal_rel[:, 0], deal_rel[:, 1]).reshape(8)
    deal_oth = jnp.where(c == 0, deal_rel[:, 1], deal_rel[:, 0]).reshape(8)
    meta = jnp.concatenate([jnp.stack([x, c, z, y]).astype(jnp.int32), deal_own, deal_oth])

    tok = tokens.reshape(ROWS, D)
    cot = cotangent.reshape(ROWS, D)
    wcols = lax.dynamic_index_in_dim(qkv_weight.reshape(48, 3, 4, CH), x, axis=2, keepdims=False)
    wcols = wcols.reshape(48, 3 * CH)
    row = jnp.concatenate(
        [ln1_gain, ln1_bias, q_bias, v_bias, out_bias, ln2_gain, ln2_bias, proj_bias, fc_bias]
    )
    wbuf = jnp.concatenate([wcols, row[None, :], jnp.zeros((7, 3 * CH), BF16)], axis=0)
    wqkv = lax.all_to_all(
        jnp.broadcast_to(wbuf, (16, 56, 3 * CH)), ("z", "y"), split_axis=0, concat_axis=0, tiled=True
    )
    tok_own = gather4(tok, "x")
    tok_oth = [swap(t) for t in tok_own]
    rows16 = wqkv[:, 48, :].astype(F32)
    vec = rows16[:, :384].reshape(16, 8, 48).transpose(1, 0, 2).reshape(8, D)
    fcb = rows16[:, 384:].reshape(1, FF)
    qvb = lax.dynamic_index_in_dim(vec[2:4].reshape(2, 4, CH), x, axis=1, keepdims=False)
    qvb = jnp.concatenate([qvb, jnp.zeros((6, CH), F32)], axis=0)

    half = lambda w, n: lax.dynamic_slice_in_dim(w, c * n, n, axis=0)
    part = jnp.concatenate(
        [half(fc_weight, 96), half(proj_weight, 96), out_weight],
        axis=0,
    )
    wall = lax.all_gather(part, ("z", "y"), axis=0, tiled=True).reshape(16, 240, D)
    fcb = lax.dynamic_index_in_dim(fcb.reshape(16, 2, 96), c, axis=1, keepdims=False)
    fcb = fcb.reshape(2, 1, D)
    cot_oth = swap(cot)

    fwd = call(
        forward_kernel,
        [shp(ROWS, CH)] * 4
        + [
            shp(8, HC, HD, BT, dtype=F32),
            shp(8, 8, BT, dtype=F32),
            shp(HC, 1024, HD),
            shp(HC, SEQ, HD),
            shp(HC, HD, SEQ),
            shp(HC, SEQ, HD),
            shp(1024, D),
            shp(D, 3 * CH),
        ],
        [pltpu.VMEM((HC, HD, SEQ), BF16)],
        us=25,
        name="attention_forward",
    )(meta, *tok_own, *tok_oth, wqkv, vec, qvb)
    att, (attt, lse, q, kk, kt, v, normed, w) = fwd[:4], fwd[4:]
    wall, first = lax.optimization_barrier((wall, att[0]))
    att = [first, *att[1:]]
    att_rel = [att[0]] + [shift(att[k], "x", -k) for k in (1, 2, 3)]

    whole = lambda *dims: pl.BlockSpec(dims, lambda j: (0,) * len(dims))
    smem = pl.BlockSpec(memory_space=pltpu.SMEM)
    hbm = pl.BlockSpec(memory_space=pl.ANY)
    wout = pl.BlockSpec((16, 48, D), lambda j: (0, 4, 0))
    mid_outs = [
        shp(ROWS, D, dtype=F32),
        shp(ROWS, D, dtype=F32),
        shp(ROWS, 1, dtype=F32),
        shp(ROWS, D),
    ]
    middle, xhat, root, n2 = pl.pallas_call(
        middle_kernel,
        grid=(1,),
        out_shape=mid_outs,
        in_specs=[smem] + [whole(ROWS, CH)] * 4 + [whole(ROWS, D), wout, whole(8, D)],
        out_specs=[whole(*o.shape) for o in mid_outs],
        compiler_params=pltpu.CompilerParams(vmem_limit_bytes=56 * 2**20),
        cost_estimate=cost(4),
        name="middle",
    )(meta, *att_rel, tok, wall, vec)
    n2_oth = swap(n2)

    mlp_outs = [
        shp(ROWS, D, dtype=F32),
        shp(ROWS, D),
        shp(ROWS, D, dtype=F32),
        shp(ROWS, D),
        shp(16, 240, D),
        shp(2, 1, D, dtype=F32),
    ]
    mlp_specs = [whole(*o.shape) for o in mlp_outs]
    mlp_specs[4] = pl.BlockSpec((8, 240, D), lambda j: (j, 0, 0))
    ffn_own, ffn_oth, dn_own, dn_oth, dw, fcg = pl.pallas_call(
        mlp_kernel,
        grid=(2,),
        out_shape=mlp_outs,
        in_specs=[whole(ROWS, D)] * 4
        + [whole(2, 1, D), pl.BlockSpec((8, 240, D), lambda j: (j, 0, 0))],
        out_specs=mlp_specs,
        scratch_shapes=[pltpu.VMEM((2 * ROWS, D), F32), pltpu.VMEM((2 * ROWS, D), F32)],
        compiler_params=pltpu.CompilerParams(vmem_limit_bytes=56 * 2**20),
        cost_estimate=cost(18),
        name="feed_forward",
    )(n2, n2_oth, cot, cot_oth, fcb, wall)
    dn_recv = swap(dn_oth)
    ffn_recv = swap(ffn_oth)
    outcome = (middle + (ffn_own + ffn_recv.astype(F32)) + vec[7:8]).astype(BF16)

    grad_outs = [shp(ROWS, D, dtype=F32)] + [shp(ROWS, CH)] * 4 + [shp(8, D, dtype=F32)]
    gm, *datt, vg2, dw = pl.pallas_call(
        middle_grad_kernel,
        grid=(1,),
        out_shape=grad_outs + [shp(16, 240, D)],
        in_specs=[smem, hbm]
        + [whole(ROWS, CH)] * 4
        + [whole(ROWS, D), wout, whole(8, D), whole(ROWS, D), whole(ROWS, 1)]
        + [whole(ROWS, D)] * 2,
        out_specs=[whole(*o.shape) for o in grad_outs] + [hbm],
        scratch_shapes=[pltpu.VMEM((16, 48, D), BF16), pltpu.SemaphoreType.DMA],
        input_output_aliases={1: 6},
        compiler_params=pltpu.CompilerParams(vmem_limit_bytes=56 * 2**20),
        cost_estimate=cost(5),
        name="middle_grad",
    )(meta, dw, *att_rel, cot, wall, vec, xhat, root, dn_own, dn_recv)
    shard_grad = lax.psum_scatter(
        dw.reshape(16 * 240, D), ("z", "y"), scatter_dimension=0, tiled=True
    )

    datt_rel = [datt[0]] + [shift(datt[k], "x", k) for k in (1, 2, 3)]
    dq, dkv_own, dkv_oth = call(
        backward_kernel,
        [shp(1024, CH), shp(1024, 2 * CH, dtype=F32), shp(1024, 2 * CH)],
        [
            pltpu.VMEM((HC, SEQ, HD), F32),
            pltpu.VMEM((HC, SEQ, HD), F32),
            pltpu.VMEM((HC, 1024, HD), BF16),
        ],
        us=24,
        name="attention_backward",
    )(meta, *datt_rel, q, kk, kt, v, attt, lse)
    dkv_recv = swap(dkv_oth)

    ng0, ng1, ng2, ng3, g = call(
        input_grad_kernel,
        [shp(ROWS, D)] * 4 + [shp(1024, 3 * CH)],
        smem=False,
        us=5,
        name="input_grad",
    )(dq, dkv_own, dkv_recv, w)
    ng_rel = [ng0] + [shift(n, "x", -k) for k, n in ((1, ng1), (2, ng2), (3, ng3))]
    wq = call(
        weight_grad_kernel,
        shp(16, 64, 3 * CH),
        [
            pltpu.VMEM((8, D), F32),
            pltpu.VMEM((16, 16, 3 * CH), F32),
        ],
        us=8,
        name="weight_grad",
    )(meta, normed, g, *tok_own, ng0, ng1, ng2, ng3, vg2, fcg)
    wq = lax.all_to_all(wq, ("z", "y"), split_axis=0, concat_axis=0, tiled=True)
    wq, *ng_rel = lax.optimization_barrier((wq, *ng_rel))
    token_grad = call(
        token_grad_kernel, shp(ROWS, D, dtype=F32), smem=False, us=3, name="token_grad"
    )(tok, gm, vec, *ng_rel)
    wq = jnp.sum(wq.astype(F32), axis=0).astype(BF16)
    wq, shard_grad = lax.optimization_barrier((wq, shard_grad))
    shard_grad = sum4([v.astype(F32) for v in gather4(shard_grad, "x")]).astype(BF16)
    wq_all = lax.all_to_all(
        jnp.broadcast_to(wq, (4, 64, 3 * CH)), "x", split_axis=0, concat_axis=0, tiled=True
    )
    wq_all = wq_all.astype(F32) + swap(wq_all).astype(F32)
    vrow = sum4([wq_all[k, 48] for k in range(4)])
    grad_qkv = wq_all[:, :48]
    grad_qkv = grad_qkv.reshape(4, 48, 3, CH).transpose(1, 2, 0, 3).reshape(48, 3 * D)
    shard_oth = swap(shard_grad).astype(F32)
    shard_grad = shard_grad.astype(F32)
    low = jnp.where(c == 0, shard_grad, shard_oth)
    high = jnp.where(c == 0, shard_oth, shard_grad)
    grad_fc_w = jnp.concatenate([low[0:96], high[0:96]], axis=0)
    grad_proj_w = jnp.concatenate([low[96:192], high[96:192]], axis=0)
    grad_out_w = shard_grad[192:] + shard_oth[192:]

    vecs = [vrow[k * 48 : (k + 1) * 48] for k in range(8)]
    return (
        outcome.reshape(tokens.shape),
        token_grad.reshape(tokens.shape),
        grad_qkv,
        vecs[0],
        vecs[1],
        vecs[2],
        vecs[3],
        grad_out_w,
        vecs[4],
        vecs[5],
        vecs[6],
        grad_fc_w,
        vrow[384:],
        grad_proj_w,
        vecs[7],
    )


def solution(mesh):
    split = Mesh(mesh.devices.reshape(4, 2, 4, 4), ("x", "core", "z", "y"))
    fsdp = ("z", "y")
    ctx = ("x", "core")
    act = P(fsdp, ctx, None, None)
    mat = P(fsdp, None)
    one = P(fsdp)
    return jax.shard_map(
        body,
        mesh=split,
        in_specs=(act, mat, mat, one, one, one, one, mat, one, one, one, mat, one, mat, one, act),
        out_specs=(act, act, mat, one, one, one, one, mat, one, one, one, mat, one, mat, one),
        check_vma=False,
    )
```

```python
import jax
import jax.numpy as jnp
from jax import lax
from jax.experimental import pallas as pl
from jax.experimental.pallas import tpu as pltpu
from jax.sharding import Mesh, PartitionSpec as P

D = 768
FF = 3072
HC = 3
HD = 64
CH = HC * HD
BT = 128
SEQ = 2048
ROWS = 256
KC = 1024
EPS = 1e-05
NEG = -1e30
F32 = jnp.float32
BF16 = jnp.bfloat16

NT = (((1,), (1,)), ((), ()))
TN = (((0,), (0,)), ((), ()))


def dot(a, b):
    return jnp.dot(a, b, preferred_element_type=F32)


def dot_nt(a, b):
    return lax.dot_general(a, b, NT, preferred_element_type=F32)


def dot_tn(a, b):
    return lax.dot_general(a, b, TN, preferred_element_type=F32)


def standardize(v):
    centre = v - jnp.mean(v, axis=-1, keepdims=True)
    spread = jnp.mean(centre * centre, axis=-1, keepdims=True)
    root = lax.rsqrt(spread + EPS)
    return centre * root, root


def rel(a, b):
    return lax.rem(a - b + 4, 4)


def forward_kernel(meta, *refs):
    toks = refs[0:8]
    wall, vec, qvb = refs[8:11]
    (atts, attt_ref, lse_ref, q_ref, k_ref, kt_ref, v_ref, normed_ref, w_ref) = (
        refs[11:15],
        *refs[15:23],
    )
    vt_ref = refs[23]
    for s in range(16):
        w_ref[s * 48 : (s + 1) * 48, :] = wall[s, 0:48, :]
    gain = vec[0:1, :]
    bias = vec[1:2, :]
    qb = qvb[0:1, :]
    vb = qvb[1:2, :]
    w = w_ref[...]
    for k in range(8):
        own = k < 4
        xhat, _ = standardize(toks[k][...].astype(F32))
        normed = (xhat * gain + bias).astype(BF16)
        if own:
            normed_ref[k * ROWS : (k + 1) * ROWS, :] = normed
            proj = dot(normed, w)
            q = (proj[:, :CH] + qb).astype(BF16) * jnp.asarray(HD**-0.5, BF16)
            for h in range(HC):
                q_ref[h, k * ROWS : (k + 1) * ROWS, :] = q[:, h * HD : (h + 1) * HD]
            kv = proj[:, CH:]
        else:
            kv = dot(normed, w[:, CH:])
        for r in range(2):
            place = pl.multiple_of(meta[4 + 2 * k + r] * BT, BT)
            kk = kv[r * BT : (r + 1) * BT, :CH]
            vv = kv[r * BT : (r + 1) * BT, CH:] + vb
            kb = kk.astype(BF16)
            vbl = vv.astype(BF16)
            for h in range(HC):
                cols = slice(h * HD, (h + 1) * HD)
                k_ref[h, pl.ds(place, BT), :] = kb[:, cols]
                v_ref[h, pl.ds(place, BT), :] = vbl[:, cols]
                kt_ref[h, :, pl.ds(place, BT)] = kk[:, cols].T.astype(BF16)
                vt_ref[h, :, pl.ds(place, BT)] = vv[:, cols].T.astype(BF16)

    key_iota = lax.broadcasted_iota(jnp.int32, (KC, BT), 0)
    query_iota = lax.broadcasted_iota(jnp.int32, (KC, BT), 1)
    for i in range(8):
        pos = meta[4 + i]
        queries = [q_ref[h, i * BT : (i + 1) * BT, :] for h in range(HC)]

        def step(j, carry, masked, pos=pos, queries=queries):
            base = pl.multiple_of(j * KC, KC)
            out = []
            if masked:
                keep = key_iota + base <= query_iota + pos * BT
            for h in range(HC):
                m, total, acc = carry[h]
                s = dot_nt(k_ref[h, pl.ds(base, KC), :], queries[h])
                if masked:
                    s = jnp.where(keep, s, NEG)
                m_new = jnp.maximum(m, jnp.max(s, axis=0, keepdims=True))
                e = jnp.exp(s - m_new)
                a = jnp.exp(m - m_new)
                total = total * a + jnp.sum(e, axis=0, keepdims=True)
                acc = acc * a + dot(vt_ref[h, :, pl.ds(base, KC)], e.astype(BF16))
                out.append((m_new, total, acc))
            return tuple(out)

        full = lax.div(pos * BT, KC)
        carry = tuple(
            (jnp.full((1, BT), NEG, F32), jnp.zeros((1, BT), F32), jnp.zeros((HD, BT), F32))
            for _ in range(HC)
        )
        carry = lax.fori_loop(0, full, lambda j, c: step(j, c, False), carry)
        carry = step(full, carry, True)
        parts = []
        for h in range(HC):
            m, total, acc = carry[h]
            att = acc / total
            attt_ref[i, h] = att
            lse_ref[i, h : h + 1, :] = m + jnp.log(total)
            parts.append(att.T.astype(BF16))
        for h in range(HC):
            atts[i // 2][(i % 2) * BT : (i % 2 + 1) * BT, h * HD : (h + 1) * HD] = parts[h]


def gelu_parts(v):
    c = 0.7978845608028654
    t = jnp.tanh(c * (v + 0.044715 * (v * v * v)))
    act = 0.5 * v * (1.0 + t)
    slope = 0.5 * (1.0 + t) + (0.5 * c) * v * (1.0 - t * t) * (1.0 + (3 * 0.044715) * v * v)
    return act, slope


def head_rows(wout, x, k):
    return wout[pl.ds(lax.rem(x + k, 4) * 4, 4)].reshape(CH, D)


def middle_kernel(meta, a0, a1, a2, a3, tok, wout, vec, middle_ref, xhat_ref, root_ref, n2_ref):
    middle = tok[...].astype(F32)
    for k, a in enumerate((a0, a1, a2, a3)):
        middle = middle + dot(a[...], head_rows(wout, meta[0], k))
    middle = middle + vec[4:5, :]
    xhat, root = standardize(middle)
    middle_ref[...] = middle
    xhat_ref[...] = xhat
    root_ref[...] = root
    n2_ref[...] = (xhat * vec[5:6, :] + vec[6:7, :]).astype(BF16)


def mlp_kernel(
    n2_own, n2_oth, cot_own, cot_oth, fcb, wblk, ffn_own, ffn_oth, dn_own, dn_oth, dw_ref, fcg_ref, ffn_s, dn_s
):
    j = pl.program_id(0)
    fc = wblk[:, 0:96, :].reshape(D, D)
    proj = wblk[:, 96:192, :].reshape(D, D)
    n2 = jnp.concatenate([n2_own[...], n2_oth[...]], axis=0)
    ct = jnp.concatenate([cot_own[...], cot_oth[...]], axis=0)
    act, slope = gelu_parts(dot_nt(n2, fc) + fcb[j])
    act = act.astype(BF16)
    gh = (dot_nt(ct, proj) * slope).astype(BF16)
    ffn = dot(act, proj)
    dn = dot(gh, fc)
    fcg_ref[j] = jnp.sum(gh.astype(F32), axis=0, keepdims=True)
    dw_ref[:, 0:96, :] = dot_tn(gh, n2).astype(BF16).reshape(8, 96, D)
    dw_ref[:, 96:192, :] = dot_tn(act, ct).astype(BF16).reshape(8, 96, D)

    @pl.when(j == 0)
    def _():
        ffn_s[...] = ffn
        dn_s[...] = dn

    @pl.when(j == 1)
    def _():
        ffn_own[...] = ffn_s[:ROWS] + ffn[:ROWS]
        ffn_oth[...] = (ffn_s[ROWS:] + ffn[ROWS:]).astype(BF16)
        dn_own[...] = dn_s[:ROWS] + dn[:ROWS]
        dn_oth[...] = (dn_s[ROWS:] + dn[ROWS:]).astype(BF16)


def middle_grad_kernel(
    meta,
    dw_in,
    a0,
    a1,
    a2,
    a3,
    cot,
    wout,
    vec,
    xhat_ref,
    root_ref,
    dn_own,
    dn_recv,
    gm_ref,
    d0,
    d1,
    d2,
    d3,
    vg_ref,
    dw_out,
    dout_s,
    sem,
):
    x = meta[0]
    ctf = cot[...].astype(F32)
    dn = dn_own[...] + dn_recv[...].astype(F32)
    xhat = xhat_ref[...]
    e = dn * vec[5:6, :]
    part = e - jnp.mean(e, axis=-1, keepdims=True)
    part = part - xhat * jnp.mean(e * xhat, axis=-1, keepdims=True)
    gm = ctf + part * root_ref[...]
    gm_ref[...] = gm
    gb = gm.astype(BF16)
    for k, (a, d) in enumerate(zip((a0, a1, a2, a3), (d0, d1, d2, d3))):
        d[...] = dot_nt(gb, head_rows(wout, x, k)).astype(BF16)
        g = dot_tn(a[...], gb).astype(BF16)
        first = lax.rem(x + k, 4) * 4
        for t in range(4):
            dout_s[first + t] = g[t * 48 : (t + 1) * 48, :]
    copy = pltpu.make_async_copy(dout_s, dw_out.at[:, 192:240, :], sem)
    copy.start()
    vg_ref[...] = jnp.concatenate(
        [
            jnp.sum(gb.astype(F32), axis=0, keepdims=True),
            jnp.sum(dn * xhat, axis=0, keepdims=True),
            jnp.sum(dn, axis=0, keepdims=True),
            jnp.sum(ctf, axis=0, keepdims=True),
            jnp.zeros((4, D), F32),
        ],
        axis=0,
    )
    copy.wait()


def backward_kernel(meta, *refs):
    dos = refs[0:4]
    q_ref, k_ref, kt_ref, v_ref, attt_ref, lse_ref = refs[4:10]
    dq_ref, own_ref, oth_ref = refs[10:13]
    dk_s, dv_s, do_s = refs[13:16]
    dk_s[...] = jnp.zeros_like(dk_s)
    dv_s[...] = jnp.zeros_like(dv_s)
    for k in range(4):
        do = dos[k][...]
        for h in range(HC):
            do_s[h, k * ROWS : (k + 1) * ROWS, :] = do[:, h * HD : (h + 1) * HD]
    key_iota = lax.broadcasted_iota(jnp.int32, (KC, BT), 0)
    query_iota = lax.broadcasted_iota(jnp.int32, (KC, BT), 1)
    for i in range(8):
        pos = meta[4 + i]
        queries = [q_ref[h, i * BT : (i + 1) * BT, :] for h in range(HC)]
        grads = [do_s[h, i * BT : (i + 1) * BT, :] for h in range(HC)]
        lses = [lse_ref[i, h : h + 1, :] for h in range(HC)]
        corrs = [
            jnp.sum(grads[h].astype(F32).T * attt_ref[i, h], axis=0, keepdims=True)
            for h in range(HC)
        ]

        def step(j, carry, masked, pos=pos, queries=queries, grads=grads, lses=lses, corrs=corrs):
            base = pl.multiple_of(j * KC, KC)
            keys = pl.ds(base, KC)
            if masked:
                keep = key_iota + base <= query_iota + pos * BT
            out = []
            for h in range(HC):
                s = dot_nt(k_ref[h, keys, :], queries[h])
                p = jnp.exp(s - lses[h])
                if masked:
                    p = jnp.where(keep, p, 0.0)
                dp = dot_nt(v_ref[h, keys, :], grads[h])
                ds = (p * (dp - corrs[h])).astype(BF16)
                dv_s[h, keys, :] += dot(p.astype(BF16), grads[h])
                dk_s[h, keys, :] += dot(ds, queries[h])
                out.append(carry[h] + dot(kt_ref[h, :, keys], ds))
            return tuple(out)

        full = lax.div(pos * BT, KC)
        carry = tuple(jnp.zeros((HD, BT), F32) for _ in range(HC))
        carry = lax.fori_loop(0, full, lambda j, c: step(j, c, False), carry)
        carry = step(full, carry, True)
        for h in range(HC):
            dq_ref[i * BT : (i + 1) * BT, h * HD : (h + 1) * HD] = (
                (carry[h] * HD**-0.5).T.astype(BF16)
            )
    for i in range(8):
        here = pl.ds(pl.multiple_of(meta[4 + i] * BT, BT), BT)
        there = pl.ds(pl.multiple_of(meta[12 + i] * BT, BT), BT)
        rows = slice(i * BT, (i + 1) * BT)
        for h in range(HC):
            own_ref[rows, h * HD : (h + 1) * HD] = dk_s[h, here, :]
            own_ref[rows, CH + h * HD : CH + (h + 1) * HD] = dv_s[h, here, :]
            oth_ref[rows, h * HD : (h + 1) * HD] = dk_s[h, there, :].astype(BF16)
            oth_ref[rows, CH + h * HD : CH + (h + 1) * HD] = dv_s[h, there, :].astype(BF16)


def input_grad_kernel(dq_ref, own_ref, recv_ref, w_ref, n0, n1, n2, n3, g_ref):
    g_ref[:, :CH] = dq_ref[...]
    g_ref[:, CH:] = (own_ref[...] + recv_ref[...].astype(F32)).astype(BF16)
    w = w_ref[...]
    for k, n in enumerate((n0, n1, n2, n3)):
        n[...] = dot_nt(g_ref[k * ROWS : (k + 1) * ROWS, :], w).astype(BF16)


def weight_grad_kernel(
    meta, normed_ref, g_ref, t0, t1, t2, t3, n0, n1, n2, n3, vg2, fcg, grad_ref, vec_s, row_s
):
    x, c = meta[0], meta[1]
    g = g_ref[...]
    grad_ref[:, 0:48, :] = dot_tn(normed_ref[...], g).astype(BF16).reshape(16, 48, HC * CH)
    gain = jnp.zeros((1, D), F32)
    bias = jnp.zeros((1, D), F32)
    for t, n in zip((t0, t1, t2, t3), (n0, n1, n2, n3)):
        xhat, _ = standardize(t[...].astype(F32))
        ng = n[...].astype(F32)
        gain = gain + jnp.sum(ng * xhat, axis=0, keepdims=True)
        bias = bias + jnp.sum(ng, axis=0, keepdims=True)
    sums = jnp.sum(g.astype(F32), axis=0, keepdims=True)
    vec_s[0:1, :] = gain
    vec_s[1:2, :] = bias
    vec_s[2:4, :] = jnp.zeros((2, D), F32)
    for i in range(4):

        @pl.when(x == i)
        def _():
            vec_s[2:3, i * CH : (i + 1) * CH] = sums[:, :CH]
            vec_s[3:4, i * CH : (i + 1) * CH] = sums[:, 2 * CH :]

    vec_s[4:8, :] = vg2[0:4, :]
    row_s[...] = jnp.zeros_like(row_s)
    for s in range(16):
        for v in range(8):
            row_s[s, 0:1, v * 48 : (v + 1) * 48] = vec_s[v : v + 1, s * 48 : (s + 1) * 48]

        @pl.when(c == 0)
        def _():
            row_s[s, 0:1, 384:480] = fcg[s // 8, :, (s % 8) * 96 : (s % 8 + 1) * 96]

        @pl.when(c == 1)
        def _():
            row_s[s, 0:1, 480:576] = fcg[s // 8, :, (s % 8) * 96 : (s % 8 + 1) * 96]

    for s in range(16):
        grad_ref[s, 48:64, :] = row_s[s].astype(BF16)


def token_grad_kernel(tok, gm, vec, n0, n1, n2, n3, out_ref):
    ng = n0[...].astype(F32) + n1[...].astype(F32) + n2[...].astype(F32) + n3[...].astype(F32)
    xhat, root = standardize(tok[...].astype(F32))
    e = ng * vec[0:1, :]
    part = e - jnp.mean(e, axis=-1, keepdims=True)
    part = part - xhat * jnp.mean(e * xhat, axis=-1, keepdims=True)
    out_ref[...] = gm[...] + part * root


def shift(v, axis, k):
    return lax.ppermute(v, axis, [(i, (i + k) % 4) for i in range(4)])


def swap(v):
    return lax.ppermute(v, "core", [(0, 1), (1, 0)])


def gather4(v, axis):
    return [v] + [shift(v, axis, k) for k in (1, 2, 3)]


def scatter4(pieces, axis):
    total = pieces[0].astype(F32)
    for k in (1, 2, 3):
        total = total + shift(pieces[k], axis, k).astype(F32)
    return total.astype(BF16)


def sum4(pieces):
    return (pieces[0] + pieces[2]) + (pieces[1] + pieces[3])


def in_order(pieces, index):
    up = [pieces[0], pieces[3], pieces[2], pieces[1]]
    twice = jnp.stack(up + up)
    return lax.dynamic_slice_in_dim(twice, rel(0, index), 4, axis=0)


def call(kernel, outs, scratch=(), smem=True, us=0, **kw):
    specs = [pl.BlockSpec(memory_space=pltpu.VMEM)]

    def run(*args):
        first = [pl.BlockSpec(memory_space=pltpu.SMEM)] if smem else specs
        return pl.pallas_call(
            kernel,
            out_shape=outs,
            in_specs=first + specs * (len(args) - 1),
            out_specs=jax.tree.map(lambda _: specs[0], outs),
            scratch_shapes=list(scratch),
            compiler_params=pltpu.CompilerParams(vmem_limit_bytes=56 * 2**20),
            cost_estimate=cost(us),
            **kw,
        )(*args)

    return run


def cost(us):
    return pl.CostEstimate(flops=us * 2 * 10**8, bytes_accessed=us * 2 * 10**5, transcendentals=0)


def shp(*dims, dtype=BF16):
    return jax.ShapeDtypeStruct(dims, dtype)


def body(
    tokens,
    dealing,
    qkv_weight,
    ln1_gain,
    ln1_bias,
    q_bias,
    v_bias,
    out_weight,
    out_bias,
    ln2_gain,
    ln2_bias,
    fc_weight,
    fc_bias,
    proj_weight,
    proj_bias,
    cotangent,
):
    x = lax.axis_index("x")
    c = lax.axis_index("core")
    z = lax.axis_index("z")
    y = lax.axis_index("y")
    deal = dealing[0].reshape(4, 2, 2)
    deal_rel = in_order([deal[0], deal[3], deal[2], deal[1]], rel(0, x))
    deal_rel = jnp.stack([deal_rel[0], deal_rel[3], deal_rel[2], deal_rel[1]])
    deal_own = jnp.where(c == 0, deal_rel[:, 0], deal_rel[:, 1]).reshape(8)
    deal_oth = jnp.where(c == 0, deal_rel[:, 1], deal_rel[:, 0]).reshape(8)
    meta = jnp.concatenate([jnp.stack([x, c, z, y]).astype(jnp.int32), deal_own, deal_oth])

    tok = tokens.reshape(ROWS, D)
    cot = cotangent.reshape(ROWS, D)
    wcols = lax.dynamic_index_in_dim(qkv_weight.reshape(48, 3, 4, CH), x, axis=2, keepdims=False)
    wcols = wcols.reshape(48, 3 * CH)
    row = jnp.concatenate(
        [ln1_gain, ln1_bias, q_bias, v_bias, out_bias, ln2_gain, ln2_bias, proj_bias, fc_bias]
    )
    wbuf = jnp.concatenate([wcols, row[None, :], jnp.zeros((7, 3 * CH), BF16)], axis=0)
    wqkv = lax.all_to_all(
        jnp.broadcast_to(wbuf, (16, 56, 3 * CH)), ("z", "y"), split_axis=0, concat_axis=0, tiled=True
    )
    tok_own = gather4(tok, "x")
    tok_oth = [swap(t) for t in tok_own]
    rows16 = wqkv[:, 48, :].astype(F32)
    vec = rows16[:, :384].reshape(16, 8, 48).transpose(1, 0, 2).reshape(8, D)
    fcb = rows16[:, 384:].reshape(1, FF)
    qvb = lax.dynamic_index_in_dim(vec[2:4].reshape(2, 4, CH), x, axis=1, keepdims=False)
    qvb = jnp.concatenate([qvb, jnp.zeros((6, CH), F32)], axis=0)

    half = lambda w, n: lax.dynamic_slice_in_dim(w, c * n, n, axis=0)
    part = jnp.concatenate(
        [half(fc_weight, 96), half(proj_weight, 96), out_weight],
        axis=0,
    )
    wall = lax.all_gather(part, ("z", "y"), axis=0, tiled=True).reshape(16, 240, D)
    fcb = lax.dynamic_index_in_dim(fcb.reshape(16, 2, 96), c, axis=1, keepdims=False)
    fcb = fcb.reshape(2, 1, D)
    cot_oth = swap(cot)

    fwd = call(
        forward_kernel,
        [shp(ROWS, CH)] * 4
        + [
            shp(8, HC, HD, BT, dtype=F32),
            shp(8, 8, BT, dtype=F32),
            shp(HC, 1024, HD),
            shp(HC, SEQ, HD),
            shp(HC, HD, SEQ),
            shp(HC, SEQ, HD),
            shp(1024, D),
            shp(D, 3 * CH),
        ],
        [pltpu.VMEM((HC, HD, SEQ), BF16)],
        us=25,
        name="attention_forward",
    )(meta, *tok_own, *tok_oth, wqkv, vec, qvb)
    att, (attt, lse, q, kk, kt, v, normed, w) = fwd[:4], fwd[4:]
    wall, first = lax.optimization_barrier((wall, att[0]))
    att = [first, *att[1:]]
    att_rel = [att[0]] + [shift(att[k], "x", -k) for k in (1, 2, 3)]

    whole = lambda *dims: pl.BlockSpec(dims, lambda j: (0,) * len(dims))
    smem = pl.BlockSpec(memory_space=pltpu.SMEM)
    hbm = pl.BlockSpec(memory_space=pl.ANY)
    wout = pl.BlockSpec((16, 48, D), lambda j: (0, 4, 0))
    mid_outs = [
        shp(ROWS, D, dtype=F32),
        shp(ROWS, D, dtype=F32),
        shp(ROWS, 1, dtype=F32),
        shp(ROWS, D),
    ]
    middle, xhat, root, n2 = pl.pallas_call(
        middle_kernel,
        grid=(1,),
        out_shape=mid_outs,
        in_specs=[smem] + [whole(ROWS, CH)] * 4 + [whole(ROWS, D), wout, whole(8, D)],
        out_specs=[whole(*o.shape) for o in mid_outs],
        compiler_params=pltpu.CompilerParams(vmem_limit_bytes=56 * 2**20),
        cost_estimate=cost(4),
        name="middle",
    )(meta, *att_rel, tok, wall, vec)
    n2_oth = swap(n2)

    mlp_outs = [
        shp(ROWS, D, dtype=F32),
        shp(ROWS, D),
        shp(ROWS, D, dtype=F32),
        shp(ROWS, D),
        shp(16, 240, D),
        shp(2, 1, D, dtype=F32),
    ]
    mlp_specs = [whole(*o.shape) for o in mlp_outs]
    mlp_specs[4] = pl.BlockSpec((8, 240, D), lambda j: (j, 0, 0))
    ffn_own, ffn_oth, dn_own, dn_oth, dw, fcg = pl.pallas_call(
        mlp_kernel,
        grid=(2,),
        out_shape=mlp_outs,
        in_specs=[whole(ROWS, D)] * 4
        + [whole(2, 1, D), pl.BlockSpec((8, 240, D), lambda j: (j, 0, 0))],
        out_specs=mlp_specs,
        scratch_shapes=[pltpu.VMEM((2 * ROWS, D), F32), pltpu.VMEM((2 * ROWS, D), F32)],
        compiler_params=pltpu.CompilerParams(vmem_limit_bytes=56 * 2**20),
        cost_estimate=cost(18),
        name="feed_forward",
    )(n2, n2_oth, cot, cot_oth, fcb, wall)
    dn_recv = swap(dn_oth)
    ffn_recv = swap(ffn_oth)
    outcome = (middle + (ffn_own + ffn_recv.astype(F32)) + vec[7:8]).astype(BF16)

    grad_outs = [shp(ROWS, D, dtype=F32)] + [shp(ROWS, CH)] * 4 + [shp(8, D, dtype=F32)]
    gm, *datt, vg2, dw = pl.pallas_call(
        middle_grad_kernel,
        grid=(1,),
        out_shape=grad_outs + [shp(16, 240, D)],
        in_specs=[smem, hbm]
        + [whole(ROWS, CH)] * 4
        + [whole(ROWS, D), wout, whole(8, D), whole(ROWS, D), whole(ROWS, 1)]
        + [whole(ROWS, D)] * 2,
        out_specs=[whole(*o.shape) for o in grad_outs] + [hbm],
        scratch_shapes=[pltpu.VMEM((16, 48, D), BF16), pltpu.SemaphoreType.DMA],
        input_output_aliases={1: 6},
        compiler_params=pltpu.CompilerParams(vmem_limit_bytes=56 * 2**20),
        cost_estimate=cost(5),
        name="middle_grad",
    )(meta, dw, *att_rel, cot, wall, vec, xhat, root, dn_own, dn_recv)
    shard_grad = lax.psum_scatter(
        dw.reshape(16 * 240, D), ("z", "y"), scatter_dimension=0, tiled=True
    )

    datt_rel = [datt[0]] + [shift(datt[k], "x", k) for k in (1, 2, 3)]
    dq, dkv_own, dkv_oth = call(
        backward_kernel,
        [shp(1024, CH), shp(1024, 2 * CH, dtype=F32), shp(1024, 2 * CH)],
        [
            pltpu.VMEM((HC, SEQ, HD), F32),
            pltpu.VMEM((HC, SEQ, HD), F32),
            pltpu.VMEM((HC, 1024, HD), BF16),
        ],
        us=24,
        name="attention_backward",
    )(meta, *datt_rel, q, kk, kt, v, attt, lse)
    dkv_recv = swap(dkv_oth)

    ng0, ng1, ng2, ng3, g = call(
        input_grad_kernel,
        [shp(ROWS, D)] * 4 + [shp(1024, 3 * CH)],
        smem=False,
        us=5,
        name="input_grad",
    )(dq, dkv_own, dkv_recv, w)
    ng_rel = [ng0] + [shift(n, "x", -k) for k, n in ((1, ng1), (2, ng2), (3, ng3))]
    wq = call(
        weight_grad_kernel,
        shp(16, 64, 3 * CH),
        [
            pltpu.VMEM((8, D), F32),
            pltpu.VMEM((16, 16, 3 * CH), F32),
        ],
        us=8,
        name="weight_grad",
    )(meta, normed, g, *tok_own, ng0, ng1, ng2, ng3, vg2, fcg)
    wq = lax.all_to_all(wq, ("z", "y"), split_axis=0, concat_axis=0, tiled=True)
    token_grad = call(
        token_grad_kernel, shp(ROWS, D, dtype=F32), smem=False, us=3, name="token_grad"
    )(tok, gm, vec, *ng_rel)
    wq, token_grad = lax.optimization_barrier((wq, token_grad))
    wq = jnp.sum(wq.astype(F32), axis=0).astype(BF16)
    wq, shard_grad = lax.optimization_barrier((wq, shard_grad))
    shard_grad = sum4([v.astype(F32) for v in gather4(shard_grad, "x")]).astype(BF16)
    wq_all = lax.all_to_all(
        jnp.broadcast_to(wq, (4, 64, 3 * CH)), "x", split_axis=0, concat_axis=0, tiled=True
    )
    wq_all = wq_all.astype(F32) + swap(wq_all).astype(F32)
    vrow = sum4([wq_all[k, 48] for k in range(4)])
    grad_qkv = wq_all[:, :48]
    grad_qkv = grad_qkv.reshape(4, 48, 3, CH).transpose(1, 2, 0, 3).reshape(48, 3 * D)
    shard_oth = swap(shard_grad).astype(F32)
    shard_grad = shard_grad.astype(F32)
    low = jnp.where(c == 0, shard_grad, shard_oth)
    high = jnp.where(c == 0, shard_oth, shard_grad)
    grad_fc_w = jnp.concatenate([low[0:96], high[0:96]], axis=0)
    grad_proj_w = jnp.concatenate([low[96:192], high[96:192]], axis=0)
    grad_out_w = shard_grad[192:] + shard_oth[192:]

    vecs = [vrow[k * 48 : (k + 1) * 48] for k in range(8)]
    return (
        outcome.reshape(tokens.shape),
        token_grad.reshape(tokens.shape),
        grad_qkv,
        vecs[0],
        vecs[1],
        vecs[2],
        vecs[3],
        grad_out_w,
        vecs[4],
        vecs[5],
        vecs[6],
        grad_fc_w,
        vrow[384:],
        grad_proj_w,
        vecs[7],
    )


def solution(mesh):
    split = Mesh(mesh.devices.reshape(4, 2, 4, 4), ("x", "core", "z", "y"))
    fsdp = ("z", "y")
    ctx = ("x", "core")
    act = P(fsdp, ctx, None, None)
    mat = P(fsdp, None)
    one = P(fsdp)
    return jax.shard_map(
        body,
        mesh=split,
        in_specs=(act, mat, mat, one, one, one, one, mat, one, one, one, mat, one, mat, one, act),
        out_specs=(act, act, mat, one, one, one, one, mat, one, one, one, mat, one, mat, one),
        check_vma=False,
    )
```

```python
import jax
import jax.numpy as jnp
from jax import lax
from jax.experimental import pallas as pl
from jax.experimental.pallas import tpu as pltpu
from jax.sharding import Mesh, PartitionSpec as P

D = 768
FF = 3072
HC = 3
HD = 64
CH = HC * HD
BT = 128
SEQ = 2048
ROWS = 256
KC = 1024
EPS = 1e-05
NEG = -1e30
F32 = jnp.float32
BF16 = jnp.bfloat16

NT = (((1,), (1,)), ((), ()))
TN = (((0,), (0,)), ((), ()))


def dot(a, b):
    return jnp.dot(a, b, preferred_element_type=F32)


def dot_nt(a, b):
    return lax.dot_general(a, b, NT, preferred_element_type=F32)


def dot_tn(a, b):
    return lax.dot_general(a, b, TN, preferred_element_type=F32)


def standardize(v):
    centre = v - jnp.mean(v, axis=-1, keepdims=True)
    spread = jnp.mean(centre * centre, axis=-1, keepdims=True)
    root = lax.rsqrt(spread + EPS)
    return centre * root, root


def rel(a, b):
    return lax.rem(a - b + 4, 4)


def forward_kernel(meta, *refs):
    toks = refs[0:8]
    wall, vec, qvb = refs[8:11]
    (atts, attt_ref, lse_ref, q_ref, k_ref, kt_ref, v_ref, normed_ref, w_ref) = (
        refs[11:15],
        *refs[15:23],
    )
    vt_ref = refs[23]
    for s in range(16):
        w_ref[s * 48 : (s + 1) * 48, :] = wall[s, 0:48, :]
    gain = vec[0:1, :]
    bias = vec[1:2, :]
    qb = qvb[0:1, :]
    vb = qvb[1:2, :]
    w = w_ref[...]
    for k in range(8):
        own = k < 4
        xhat, _ = standardize(toks[k][...].astype(F32))
        normed = (xhat * gain + bias).astype(BF16)
        if own:
            normed_ref[k * ROWS : (k + 1) * ROWS, :] = normed
            proj = dot(normed, w)
            q = (proj[:, :CH] + qb).astype(BF16) * jnp.asarray(HD**-0.5, BF16)
            for h in range(HC):
                q_ref[h, k * ROWS : (k + 1) * ROWS, :] = q[:, h * HD : (h + 1) * HD]
            kv = proj[:, CH:]
        else:
            kv = dot(normed, w[:, CH:])
        for r in range(2):
            place = pl.multiple_of(meta[4 + 2 * k + r] * BT, BT)
            kk = kv[r * BT : (r + 1) * BT, :CH]
            vv = kv[r * BT : (r + 1) * BT, CH:] + vb
            kb = kk.astype(BF16)
            vbl = vv.astype(BF16)
            for h in range(HC):
                cols = slice(h * HD, (h + 1) * HD)
                k_ref[h, pl.ds(place, BT), :] = kb[:, cols]
                v_ref[h, pl.ds(place, BT), :] = vbl[:, cols]
                kt_ref[h, :, pl.ds(place, BT)] = kk[:, cols].T.astype(BF16)
                vt_ref[h, :, pl.ds(place, BT)] = vv[:, cols].T.astype(BF16)

    key_iota = lax.broadcasted_iota(jnp.int32, (KC, BT), 0)
    query_iota = lax.broadcasted_iota(jnp.int32, (KC, BT), 1)
    for i in range(8):
        pos = meta[4 + i]
        queries = [q_ref[h, i * BT : (i + 1) * BT, :] for h in range(HC)]

        def step(j, carry, masked, pos=pos, queries=queries):
            base = pl.multiple_of(j * KC, KC)
            out = []
            if masked:
                keep = key_iota + base <= query_iota + pos * BT
            for h in range(HC):
                m, total, acc = carry[h]
                s = dot_nt(k_ref[h, pl.ds(base, KC), :], queries[h])
                if masked:
                    s = jnp.where(keep, s, NEG)
                m_new = jnp.maximum(m, jnp.max(s, axis=0, keepdims=True))
                e = jnp.exp(s - m_new)
                a = jnp.exp(m - m_new)
                total = total * a + jnp.sum(e, axis=0, keepdims=True)
                acc = acc * a + dot(vt_ref[h, :, pl.ds(base, KC)], e.astype(BF16))
                out.append((m_new, total, acc))
            return tuple(out)

        full = lax.div(pos * BT, KC)
        carry = tuple(
            (jnp.full((1, BT), NEG, F32), jnp.zeros((1, BT), F32), jnp.zeros((HD, BT), F32))
            for _ in range(HC)
        )
        carry = lax.fori_loop(0, full, lambda j, c: step(j, c, False), carry)
        carry = step(full, carry, True)
        parts = []
        for h in range(HC):
            m, total, acc = carry[h]
            att = acc / total
            attt_ref[i, h] = att
            lse_ref[i, h : h + 1, :] = m + jnp.log(total)
            parts.append(att.T.astype(BF16))
        for h in range(HC):
            atts[i // 2][(i % 2) * BT : (i % 2 + 1) * BT, h * HD : (h + 1) * HD] = parts[h]


def gelu_parts(v):
    c = 0.7978845608028654
    t = jnp.tanh(c * (v + 0.044715 * (v * v * v)))
    act = 0.5 * v * (1.0 + t)
    slope = 0.5 * (1.0 + t) + (0.5 * c) * v * (1.0 - t * t) * (1.0 + (3 * 0.044715) * v * v)
    return act, slope


def head_rows(wout, x, k):
    return wout[pl.ds(lax.rem(x + k, 4) * 4, 4)].reshape(CH, D)


def middle_kernel(meta, a0, a1, a2, a3, tok, wout, vec, middle_ref, xhat_ref, root_ref, n2_ref):
    middle = tok[...].astype(F32)
    for k, a in enumerate((a0, a1, a2, a3)):
        middle = middle + dot(a[...], head_rows(wout, meta[0], k))
    middle = middle + vec[4:5, :]
    xhat, root = standardize(middle)
    middle_ref[...] = middle
    xhat_ref[...] = xhat
    root_ref[...] = root
    n2_ref[...] = (xhat * vec[5:6, :] + vec[6:7, :]).astype(BF16)


def mlp_kernel(
    n2_own, n2_oth, cot_own, cot_oth, fcb, wblk, ffn_own, ffn_oth, dn_own, dn_oth, dw_ref, fcg_ref, ffn_s, dn_s
):
    j = pl.program_id(0)
    fc = wblk[:, 0:96, :].reshape(D, D)
    proj = wblk[:, 96:192, :].reshape(D, D)
    n2 = jnp.concatenate([n2_own[...], n2_oth[...]], axis=0)
    ct = jnp.concatenate([cot_own[...], cot_oth[...]], axis=0)
    act, slope = gelu_parts(dot_nt(n2, fc) + fcb[j])
    act = act.astype(BF16)
    gh = (dot_nt(ct, proj) * slope).astype(BF16)
    ffn = dot(act, proj)
    dn = dot(gh, fc)
    fcg_ref[j] = jnp.sum(gh.astype(F32), axis=0, keepdims=True)
    dw_ref[:, 0:96, :] = dot_tn(gh, n2).astype(BF16).reshape(8, 96, D)
    dw_ref[:, 96:192, :] = dot_tn(act, ct).astype(BF16).reshape(8, 96, D)

    @pl.when(j == 0)
    def _():
        ffn_s[...] = ffn
        dn_s[...] = dn

    @pl.when(j == 1)
    def _():
        ffn_own[...] = ffn_s[:ROWS] + ffn[:ROWS]
        ffn_oth[...] = (ffn_s[ROWS:] + ffn[ROWS:]).astype(BF16)
        dn_own[...] = dn_s[:ROWS] + dn[:ROWS]
        dn_oth[...] = (dn_s[ROWS:] + dn[ROWS:]).astype(BF16)


def middle_grad_kernel(
    meta,
    dw_in,
    a0,
    a1,
    a2,
    a3,
    cot,
    wout,
    vec,
    xhat_ref,
    root_ref,
    dn_own,
    dn_recv,
    gm_ref,
    d0,
    d1,
    d2,
    d3,
    vg_ref,
    dw_out,
    dout_s,
    sem,
):
    x = meta[0]
    ctf = cot[...].astype(F32)
    dn = dn_own[...] + dn_recv[...].astype(F32)
    xhat = xhat_ref[...]
    e = dn * vec[5:6, :]
    part = e - jnp.mean(e, axis=-1, keepdims=True)
    part = part - xhat * jnp.mean(e * xhat, axis=-1, keepdims=True)
    gm = ctf + part * root_ref[...]
    gm_ref[...] = gm
    gb = gm.astype(BF16)
    for k, (a, d) in enumerate(zip((a0, a1, a2, a3), (d0, d1, d2, d3))):
        d[...] = dot_nt(gb, head_rows(wout, x, k)).astype(BF16)
        g = dot_tn(a[...], gb).astype(BF16)
        first = lax.rem(x + k, 4) * 4
        for t in range(4):
            dout_s[first + t] = g[t * 48 : (t + 1) * 48, :]
    copy = pltpu.make_async_copy(dout_s, dw_out.at[:, 192:240, :], sem)
    copy.start()
    vg_ref[...] = jnp.concatenate(
        [
            jnp.sum(gb.astype(F32), axis=0, keepdims=True),
            jnp.sum(dn * xhat, axis=0, keepdims=True),
            jnp.sum(dn, axis=0, keepdims=True),
            jnp.sum(ctf, axis=0, keepdims=True),
            jnp.zeros((4, D), F32),
        ],
        axis=0,
    )
    copy.wait()


def backward_kernel(meta, *refs):
    dos = refs[0:4]
    q_ref, k_ref, kt_ref, v_ref, attt_ref, lse_ref = refs[4:10]
    dq_ref, own_ref, oth_ref = refs[10:13]
    dk_s, dv_s, do_s = refs[13:16]
    dk_s[...] = jnp.zeros_like(dk_s)
    dv_s[...] = jnp.zeros_like(dv_s)
    for k in range(4):
        do = dos[k][...]
        for h in range(HC):
            do_s[h, k * ROWS : (k + 1) * ROWS, :] = do[:, h * HD : (h + 1) * HD]
    key_iota = lax.broadcasted_iota(jnp.int32, (KC, BT), 0)
    query_iota = lax.broadcasted_iota(jnp.int32, (KC, BT), 1)
    for i in range(8):
        pos = meta[4 + i]
        queries = [q_ref[h, i * BT : (i + 1) * BT, :] for h in range(HC)]
        grads = [do_s[h, i * BT : (i + 1) * BT, :] for h in range(HC)]
        lses = [lse_ref[i, h : h + 1, :] for h in range(HC)]
        corrs = [
            jnp.sum(grads[h].astype(F32).T * attt_ref[i, h], axis=0, keepdims=True)
            for h in range(HC)
        ]

        def step(j, carry, masked, pos=pos, queries=queries, grads=grads, lses=lses, corrs=corrs):
            base = pl.multiple_of(j * KC, KC)
            keys = pl.ds(base, KC)
            if masked:
                keep = key_iota + base <= query_iota + pos * BT
            out = []
            for h in range(HC):
                s = dot_nt(k_ref[h, keys, :], queries[h])
                p = jnp.exp(s - lses[h])
                if masked:
                    p = jnp.where(keep, p, 0.0)
                dp = dot_nt(v_ref[h, keys, :], grads[h])
                ds = (p * (dp - corrs[h])).astype(BF16)
                dv_s[h, keys, :] += dot(p.astype(BF16), grads[h])
                dk_s[h, keys, :] += dot(ds, queries[h])
                out.append(carry[h] + dot(kt_ref[h, :, keys], ds))
            return tuple(out)

        full = lax.div(pos * BT, KC)
        carry = tuple(jnp.zeros((HD, BT), F32) for _ in range(HC))
        carry = lax.fori_loop(0, full, lambda j, c: step(j, c, False), carry)
        carry = step(full, carry, True)
        for h in range(HC):
            dq_ref[i * BT : (i + 1) * BT, h * HD : (h + 1) * HD] = (
                (carry[h] * HD**-0.5).T.astype(BF16)
            )
    for i in range(8):
        here = pl.ds(pl.multiple_of(meta[4 + i] * BT, BT), BT)
        there = pl.ds(pl.multiple_of(meta[12 + i] * BT, BT), BT)
        rows = slice(i * BT, (i + 1) * BT)
        for h in range(HC):
            own_ref[rows, h * HD : (h + 1) * HD] = dk_s[h, here, :]
            own_ref[rows, CH + h * HD : CH + (h + 1) * HD] = dv_s[h, here, :]
            oth_ref[rows, h * HD : (h + 1) * HD] = dk_s[h, there, :].astype(BF16)
            oth_ref[rows, CH + h * HD : CH + (h + 1) * HD] = dv_s[h, there, :].astype(BF16)


def input_grad_kernel(dq_ref, own_ref, recv_ref, w_ref, n0, n1, n2, n3, g_ref):
    g_ref[:, :CH] = dq_ref[...]
    g_ref[:, CH:] = (own_ref[...] + recv_ref[...].astype(F32)).astype(BF16)
    w = w_ref[...]
    for k, n in enumerate((n0, n1, n2, n3)):
        n[...] = dot_nt(g_ref[k * ROWS : (k + 1) * ROWS, :], w).astype(BF16)


def weight_grad_kernel(
    meta, normed_ref, g_ref, t0, t1, t2, t3, n0, n1, n2, n3, vg2, fcg, grad_ref, vec_s, row_s
):
    x, c = meta[0], meta[1]
    g = g_ref[...]
    grad_ref[:, 0:48, :] = dot_tn(normed_ref[...], g).astype(BF16).reshape(16, 48, HC * CH)
    gain = jnp.zeros((1, D), F32)
    bias = jnp.zeros((1, D), F32)
    for t, n in zip((t0, t1, t2, t3), (n0, n1, n2, n3)):
        xhat, _ = standardize(t[...].astype(F32))
        ng = n[...].astype(F32)
        gain = gain + jnp.sum(ng * xhat, axis=0, keepdims=True)
        bias = bias + jnp.sum(ng, axis=0, keepdims=True)
    sums = jnp.sum(g.astype(F32), axis=0, keepdims=True)
    vec_s[0:1, :] = gain
    vec_s[1:2, :] = bias
    vec_s[2:4, :] = jnp.zeros((2, D), F32)
    for i in range(4):

        @pl.when(x == i)
        def _():
            vec_s[2:3, i * CH : (i + 1) * CH] = sums[:, :CH]
            vec_s[3:4, i * CH : (i + 1) * CH] = sums[:, 2 * CH :]

    vec_s[4:8, :] = vg2[0:4, :]
    row_s[...] = jnp.zeros_like(row_s)
    for s in range(16):
        for v in range(8):
            row_s[s, 0:1, v * 48 : (v + 1) * 48] = vec_s[v : v + 1, s * 48 : (s + 1) * 48]

        @pl.when(c == 0)
        def _():
            row_s[s, 0:1, 384:480] = fcg[s // 8, :, (s % 8) * 96 : (s % 8 + 1) * 96]

        @pl.when(c == 1)
        def _():
            row_s[s, 0:1, 480:576] = fcg[s // 8, :, (s % 8) * 96 : (s % 8 + 1) * 96]

    for s in range(16):
        grad_ref[s, 48:64, :] = row_s[s].astype(BF16)


def token_grad_kernel(tok, gm, vec, n0, n1, n2, n3, out_ref):
    ng = n0[...].astype(F32) + n1[...].astype(F32) + n2[...].astype(F32) + n3[...].astype(F32)
    xhat, root = standardize(tok[...].astype(F32))
    e = ng * vec[0:1, :]
    part = e - jnp.mean(e, axis=-1, keepdims=True)
    part = part - xhat * jnp.mean(e * xhat, axis=-1, keepdims=True)
    out_ref[...] = gm[...] + part * root


def shift(v, axis, k):
    return lax.ppermute(v, axis, [(i, (i + k) % 4) for i in range(4)])


def swap(v):
    return lax.ppermute(v, "core", [(0, 1), (1, 0)])


def gather4(v, axis):
    return [v] + [shift(v, axis, k) for k in (1, 2, 3)]


def scatter4(pieces, axis):
    total = pieces[0].astype(F32)
    for k in (1, 2, 3):
        total = total + shift(pieces[k], axis, k).astype(F32)
    return total.astype(BF16)


def sum4(pieces):
    return (pieces[0] + pieces[2]) + (pieces[1] + pieces[3])


def in_order(pieces, index):
    up = [pieces[0], pieces[3], pieces[2], pieces[1]]
    twice = jnp.stack(up + up)
    return lax.dynamic_slice_in_dim(twice, rel(0, index), 4, axis=0)


def call(kernel, outs, scratch=(), smem=True, us=0, **kw):
    specs = [pl.BlockSpec(memory_space=pltpu.VMEM)]

    def run(*args):
        first = [pl.BlockSpec(memory_space=pltpu.SMEM)] if smem else specs
        return pl.pallas_call(
            kernel,
            out_shape=outs,
            in_specs=first + specs * (len(args) - 1),
            out_specs=jax.tree.map(lambda _: specs[0], outs),
            scratch_shapes=list(scratch),
            compiler_params=pltpu.CompilerParams(vmem_limit_bytes=56 * 2**20),
            cost_estimate=cost(us),
            **kw,
        )(*args)

    return run


def cost(us):
    return pl.CostEstimate(flops=us * 2 * 10**8, bytes_accessed=us * 2 * 10**5, transcendentals=0)


def shp(*dims, dtype=BF16):
    return jax.ShapeDtypeStruct(dims, dtype)


def body(
    tokens,
    dealing,
    qkv_weight,
    ln1_gain,
    ln1_bias,
    q_bias,
    v_bias,
    out_weight,
    out_bias,
    ln2_gain,
    ln2_bias,
    fc_weight,
    fc_bias,
    proj_weight,
    proj_bias,
    cotangent,
):
    x = lax.axis_index("x")
    c = lax.axis_index("core")
    z = lax.axis_index("z")
    y = lax.axis_index("y")
    deal = dealing[0].reshape(4, 2, 2)
    deal_rel = in_order([deal[0], deal[3], deal[2], deal[1]], rel(0, x))
    deal_rel = jnp.stack([deal_rel[0], deal_rel[3], deal_rel[2], deal_rel[1]])
    deal_own = jnp.where(c == 0, deal_rel[:, 0], deal_rel[:, 1]).reshape(8)
    deal_oth = jnp.where(c == 0, deal_rel[:, 1], deal_rel[:, 0]).reshape(8)
    meta = jnp.concatenate([jnp.stack([x, c, z, y]).astype(jnp.int32), deal_own, deal_oth])

    tok = tokens.reshape(ROWS, D)
    cot = cotangent.reshape(ROWS, D)
    wcols = lax.dynamic_index_in_dim(qkv_weight.reshape(48, 3, 4, CH), x, axis=2, keepdims=False)
    wcols = wcols.reshape(48, 3 * CH)
    row = jnp.concatenate(
        [ln1_gain, ln1_bias, q_bias, v_bias, out_bias, ln2_gain, ln2_bias, proj_bias, fc_bias]
    )
    wbuf = jnp.concatenate([wcols, row[None, :], jnp.zeros((7, 3 * CH), BF16)], axis=0)
    wqkv = lax.all_to_all(
        jnp.broadcast_to(wbuf, (16, 56, 3 * CH)), ("z", "y"), split_axis=0, concat_axis=0, tiled=True
    )
    tok_own = gather4(tok, "x")
    tok_oth = [swap(t) for t in tok_own]
    rows16 = wqkv[:, 48, :].astype(F32)
    vec = rows16[:, :384].reshape(16, 8, 48).transpose(1, 0, 2).reshape(8, D)
    fcb = rows16[:, 384:].reshape(1, FF)
    qvb = lax.dynamic_index_in_dim(vec[2:4].reshape(2, 4, CH), x, axis=1, keepdims=False)
    qvb = jnp.concatenate([qvb, jnp.zeros((6, CH), F32)], axis=0)

    half = lambda w, n: lax.dynamic_slice_in_dim(w, c * n, n, axis=0)
    part = jnp.concatenate(
        [half(fc_weight, 96), half(proj_weight, 96), out_weight],
        axis=0,
    )
    wall = lax.all_gather(part, ("z", "y"), axis=0, tiled=True).reshape(16, 240, D)
    fcb = lax.dynamic_index_in_dim(fcb.reshape(16, 2, 96), c, axis=1, keepdims=False)
    fcb = fcb.reshape(2, 1, D)
    cot_oth = swap(cot)

    fwd = call(
        forward_kernel,
        [shp(ROWS, CH)] * 4
        + [
            shp(8, HC, HD, BT, dtype=F32),
            shp(8, 8, BT, dtype=F32),
            shp(HC, 1024, HD),
            shp(HC, SEQ, HD),
            shp(HC, HD, SEQ),
            shp(HC, SEQ, HD),
            shp(1024, D),
            shp(D, 3 * CH),
        ],
        [pltpu.VMEM((HC, HD, SEQ), BF16)],
        us=25,
        name="attention_forward",
    )(meta, *tok_own, *tok_oth, wqkv, vec, qvb)
    att, (attt, lse, q, kk, kt, v, normed, w) = fwd[:4], fwd[4:]
    wall, first = lax.optimization_barrier((wall, att[0]))
    att = [first, *att[1:]]
    att_rel = [att[0]] + [shift(att[k], "x", -k) for k in (1, 2, 3)]

    whole = lambda *dims: pl.BlockSpec(dims, lambda j: (0,) * len(dims))
    smem = pl.BlockSpec(memory_space=pltpu.SMEM)
    hbm = pl.BlockSpec(memory_space=pl.ANY)
    wout = pl.BlockSpec((16, 48, D), lambda j: (0, 4, 0))
    mid_outs = [
        shp(ROWS, D, dtype=F32),
        shp(ROWS, D, dtype=F32),
        shp(ROWS, 1, dtype=F32),
        shp(ROWS, D),
    ]
    middle, xhat, root, n2 = pl.pallas_call(
        middle_kernel,
        grid=(1,),
        out_shape=mid_outs,
        in_specs=[smem] + [whole(ROWS, CH)] * 4 + [whole(ROWS, D), wout, whole(8, D)],
        out_specs=[whole(*o.shape) for o in mid_outs],
        compiler_params=pltpu.CompilerParams(vmem_limit_bytes=56 * 2**20),
        cost_estimate=cost(4),
        name="middle",
    )(meta, *att_rel, tok, wall, vec)
    n2_oth = swap(n2)

    mlp_outs = [
        shp(ROWS, D, dtype=F32),
        shp(ROWS, D),
        shp(ROWS, D, dtype=F32),
        shp(ROWS, D),
        shp(16, 240, D),
        shp(2, 1, D, dtype=F32),
    ]
    mlp_specs = [whole(*o.shape) for o in mlp_outs]
    mlp_specs[4] = pl.BlockSpec((8, 240, D), lambda j: (j, 0, 0))
    ffn_own, ffn_oth, dn_own, dn_oth, dw, fcg = pl.pallas_call(
        mlp_kernel,
        grid=(2,),
        out_shape=mlp_outs,
        in_specs=[whole(ROWS, D)] * 4
        + [whole(2, 1, D), pl.BlockSpec((8, 240, D), lambda j: (j, 0, 0))],
        out_specs=mlp_specs,
        scratch_shapes=[pltpu.VMEM((2 * ROWS, D), F32), pltpu.VMEM((2 * ROWS, D), F32)],
        compiler_params=pltpu.CompilerParams(vmem_limit_bytes=56 * 2**20),
        cost_estimate=cost(18),
        name="feed_forward",
    )(n2, n2_oth, cot, cot_oth, fcb, wall)
    dn_recv = swap(dn_oth)
    ffn_recv = swap(ffn_oth)
    outcome = (middle + (ffn_own + ffn_recv.astype(F32)) + vec[7:8]).astype(BF16)

    grad_outs = [shp(ROWS, D, dtype=F32)] + [shp(ROWS, CH)] * 4 + [shp(8, D, dtype=F32)]
    gm, *datt, vg2, dw = pl.pallas_call(
        middle_grad_kernel,
        grid=(1,),
        out_shape=grad_outs + [shp(16, 240, D)],
        in_specs=[smem, hbm]
        + [whole(ROWS, CH)] * 4
        + [whole(ROWS, D), wout, whole(8, D), whole(ROWS, D), whole(ROWS, 1)]
        + [whole(ROWS, D)] * 2,
        out_specs=[whole(*o.shape) for o in grad_outs] + [hbm],
        scratch_shapes=[pltpu.VMEM((16, 48, D), BF16), pltpu.SemaphoreType.DMA],
        input_output_aliases={1: 6},
        compiler_params=pltpu.CompilerParams(vmem_limit_bytes=56 * 2**20),
        cost_estimate=cost(5),
        name="middle_grad",
    )(meta, dw, *att_rel, cot, wall, vec, xhat, root, dn_own, dn_recv)
    shard_grad = lax.psum_scatter(
        dw.reshape(16 * 240, D), ("z", "y"), scatter_dimension=0, tiled=True
    )

    datt_rel = [datt[0]] + [shift(datt[k], "x", k) for k in (1, 2, 3)]
    dq, dkv_own, dkv_oth = call(
        backward_kernel,
        [shp(1024, CH), shp(1024, 2 * CH, dtype=F32), shp(1024, 2 * CH)],
        [
            pltpu.VMEM((HC, SEQ, HD), F32),
            pltpu.VMEM((HC, SEQ, HD), F32),
            pltpu.VMEM((HC, 1024, HD), BF16),
        ],
        us=24,
        name="attention_backward",
    )(meta, *datt_rel, q, kk, kt, v, attt, lse)
    dkv_recv = swap(dkv_oth)

    ng0, ng1, ng2, ng3, g = call(
        input_grad_kernel,
        [shp(ROWS, D)] * 4 + [shp(1024, 3 * CH)],
        smem=False,
        us=5,
        name="input_grad",
    )(dq, dkv_own, dkv_recv, w)
    ng_rel = [ng0] + [shift(n, "x", -k) for k, n in ((1, ng1), (2, ng2), (3, ng3))]
    wq = call(
        weight_grad_kernel,
        shp(16, 64, 3 * CH),
        [
            pltpu.VMEM((8, D), F32),
            pltpu.VMEM((16, 16, 3 * CH), F32),
        ],
        us=8,
        name="weight_grad",
    )(meta, normed, g, *tok_own, ng0, ng1, ng2, ng3, vg2, fcg)
    wq = lax.all_to_all(wq, ("z", "y"), split_axis=0, concat_axis=0, tiled=True)
    token_grad = call(
        token_grad_kernel, shp(ROWS, D, dtype=F32), smem=False, us=3, name="token_grad"
    )(tok, gm, vec, *ng_rel)
    wq, token_grad = lax.optimization_barrier((wq, token_grad))
    wq = jnp.sum(wq.astype(F32), axis=0).astype(BF16)
    wq, shard_grad = lax.optimization_barrier((wq, shard_grad))
    shard_grad = sum4([v.astype(F32) for v in gather4(shard_grad, "x")]).astype(BF16)
    wq_all = lax.all_to_all(
        jnp.broadcast_to(wq, (4, 64, 3 * CH)), "x", split_axis=0, concat_axis=0, tiled=True
    )
    wq_all = wq_all.astype(F32) + swap(wq_all).astype(F32)
    vrow = sum4([wq_all[k, 48] for k in range(4)])
    grad_qkv = wq_all[:, :48]
    grad_qkv = grad_qkv.reshape(4, 48, 3, CH).transpose(1, 2, 0, 3).reshape(48, 3 * D)
    shard_grad, grad_qkv, vrow = lax.optimization_barrier((shard_grad, grad_qkv, vrow))
    shard_oth = swap(shard_grad).astype(F32)
    shard_grad = shard_grad.astype(F32)
    low = jnp.where(c == 0, shard_grad, shard_oth)
    high = jnp.where(c == 0, shard_oth, shard_grad)
    grad_fc_w = jnp.concatenate([low[0:96], high[0:96]], axis=0)
    grad_proj_w = jnp.concatenate([low[96:192], high[96:192]], axis=0)
    grad_out_w = shard_grad[192:] + shard_oth[192:]

    vecs = [vrow[k * 48 : (k + 1) * 48] for k in range(8)]
    return (
        outcome.reshape(tokens.shape),
        token_grad.reshape(tokens.shape),
        grad_qkv,
        vecs[0],
        vecs[1],
        vecs[2],
        vecs[3],
        grad_out_w,
        vecs[4],
        vecs[5],
        vecs[6],
        grad_fc_w,
        vrow[384:],
        grad_proj_w,
        vecs[7],
    )


def solution(mesh):
    split = Mesh(mesh.devices.reshape(4, 2, 4, 4), ("x", "core", "z", "y"))
    fsdp = ("z", "y")
    ctx = ("x", "core")
    act = P(fsdp, ctx, None, None)
    mat = P(fsdp, None)
    one = P(fsdp)
    return jax.shard_map(
        body,
        mesh=split,
        in_specs=(act, mat, mat, one, one, one, one, mat, one, one, one, mat, one, mat, one, act),
        out_specs=(act, act, mat, one, one, one, one, mat, one, one, one, mat, one, mat, one),
        check_vma=False,
    )
```
